32 devices in a mesh: dp: 4 (over z), seq: 4 (over y, x), mp: 2 (over core).
Axes of the slice: x: 2, y: 2, z: 4, core: 2. Of those that a mesh axis runs over, the one named last changes fastest.
Arguments:
- residual: bfloat16 [6144, 3072], P(('dp', 'seq'), 'mp'), parts along dimension 0, may hold values from -10 to 10
- queries: bfloat16 [6144, 3072], P(('dp', 'seq', 'mp')), parts along dimension 0, may hold values from -6 to 6
- keys: bfloat16 [6144, 3072], P(('dp', 'seq', 'mp')), parts along dimension 0, may hold values from -6 to 6
- values: bfloat16 [6144, 3072], P(('dp', 'seq', 'mp')), parts along dimension 0, may hold values from -6 to 6
- video_ids: int32 [6144], P(('dp', 'seq', 'mp')), parts along dimension 0, may hold values from 0 to 3, never falling along the last dimension, each value on 1 to 768 neighbouring positions
- timestep: int32 [4], P('dp'), parts along dimension 0, may hold values from 0 to 49
- modulation: float32 [50, 3, 3072], P(None, None, 'mp'), may hold values from -4 to 4
- out_weight: bfloat16 [3072, 3072], P(None, 'mp'), may hold values from -0.109375 to 0.109375
Outputs:
- hidden_out: bfloat16 [6144, 3072], P(('dp', 'seq'), 'mp'), parts along dimension 0
- mlp_input: bfloat16 [6144, 3072], P(('dp', 'seq'), 'mp'), parts along dimension 0
The draws below stay inside these ranges and needn't reach their ends.
There are 4 independent parts, one for each index of `dp`. The reference program is written for one: setup_inputs(seed, part) draws one part's arguments, and reference() takes and returns one part's arrays. A program takes and returns all parts, laid end to end along the dimension named above; an argument that names none is the same for every part. Nothing has to cross between parts.
Inputs may be any that keep to these rules, and one draw needn't show every extreme that they name: `video_ids`: video ids never fall along the tokens; each video holds 1 to 768 tokens and one holds exactly 768.
All inputs are finite; a program needn't handle non-finite values.
Results may differ from the reference program's by a relative error of at most 0.005.
Values may be sent and summed in bfloat16 or wider, within the bound.
A program may use at most 256 MiB of HBM per device.

```python
import math
import jax
import jax.numpy as jnp
import numpy as np
from jax import lax

D = 3072
HEADS = 24
HEAD_DIM = 128
NSTEP = 50
VIDEOS = 4
TOKENS = 1536


def base_field(key):
    return 1.5 * jax.random.truncated_normal(key, -4.0, 4.0, (TOKENS, D), jnp.float32)


def draw_queries(key, part):
    field = base_field(jax.random.fold_in(key, 1))
    return field.astype(jnp.bfloat16)


def draw_keys(key, part):
    field = base_field(jax.random.fold_in(key, 2))
    return field.astype(jnp.bfloat16)


def draw_residual(key, part):
    columns = jnp.arange(D, dtype=jnp.float32)
    col_scale = 3.0 ** (columns / D) * jax.random.uniform(jax.random.fold_in(key, 3), (D,), jnp.float32, 0.6, 1.6)
    row_scale = jnp.exp(jax.random.uniform(jax.random.fold_in(key, 4), (TOKENS, 1), jnp.float32, math.log(0.05), math.log(0.5)))
    field = jax.random.truncated_normal(jax.random.fold_in(key, 5), -4.0, 4.0, (TOKENS, D), jnp.float32)
    return (field * row_scale * col_scale[None, :]).astype(jnp.bfloat16)


def block_scale(rng, dims, pieces, smallest, largest):
    gain, own = 1.0, jax.random.fold_in(rng, 6)
    for axis_at, shards_of in pieces:
        heights = jnp.exp(jax.random.uniform(jax.random.fold_in(own, axis_at), (shards_of,), jnp.float32, smallest / len(pieces), largest / len(pieces)))
        gain = gain * jnp.repeat(heights, dims[axis_at] // shards_of).reshape([-1 if axis == axis_at else 1 for axis in range(len(dims))])
    return gain


def split_up(amount, total, limit, slope):
    weights = [(1 << 20) // math.isqrt(rank ** slope) + 1 for rank in range(2, amount + 1)]
    rest, given = total - limit - (amount - 1), [1] * (amount - 1)
    while rest > 0:
        candidates = [i for i in range(amount - 1) if given[i] < limit]
        whole, remaining = sum([weights[i] for i in candidates]), rest
        for i in candidates:
            extra = min(limit - given[i], max(1, remaining * weights[i] // whole), rest)
            given[i] = given[i] + extra
            rest = rest - extra
    return np.array([limit] + given)


def uneven(stream_key, number_of, total, reach, skew):
    if number_of == 2:
        one = jax.random.randint(stream_key, (), max(1, total - reach), min(reach, total - 1) + 1)
        return jnp.stack([one, total - one])
    sizes = jnp.asarray(split_up(number_of, total, reach, skew), jnp.int32)
    twos = (number_of - 1) // 2
    donor, sink = sizes[1:1 + 2 * twos:2], sizes[2:2 + 2 * twos:2]
    slack = jnp.minimum(donor - 1, reach - sink)
    moved = jax.random.randint(jax.random.fold_in(stream_key, 1), (twos,), 0, 1 << 20) % (slack + 1)
    sizes = sizes.at[1:1 + 2 * twos:2].set(donor - moved).at[2:2 + 2 * twos:2].set(sink + moved)
    return sizes[jax.random.permutation(jax.random.fold_in(stream_key, 2), number_of)]


def noise(key, extent, scale, limit, shards=(), kind=jnp.bfloat16):
    gain = block_scale(key, extent, shards, -0.22, 0.18) if shards else 1.0
    result = jax.random.normal(key, extent, jnp.float32) * scale * gain
    return jnp.minimum(jnp.maximum(result, -limit), limit).astype(kind)


def setup_inputs(seed: int = 0, part: int = 0) -> dict:
    seeds = jax.random.split(jax.random.key(seed), 9)
    part_keys = jax.random.split(jax.random.fold_in(seeds[8], part), 9)
    return {
        "residual": draw_residual(jax.random.fold_in(jax.random.fold_in(seeds[8], part), 71), part),
        "queries": draw_queries(jax.random.fold_in(jax.random.fold_in(seeds[8], part), 71), part),
        "keys": draw_keys(jax.random.fold_in(jax.random.fold_in(seeds[8], part), 71), part),
        "values": noise(part_keys[3], (TOKENS, D), 1.0, 6.0, ((0, 8),)),
        "video_ids": jnp.searchsorted(jnp.cumsum(uneven(part_keys[4], VIDEOS, TOKENS, TOKENS // 2, 2)), jnp.arange(TOKENS), side="right").astype(jnp.int32),
        "timestep": jax.random.randint(part_keys[5], (1,), 0, NSTEP).astype(jnp.int32),
        "modulation": noise(seeds[6], (NSTEP, 3, D), 1.0, 4.0, ((2, 2),), jnp.float32),
        "out_weight": noise(seeds[7], (D, D), D ** -0.5, 0.109375, ((1, 2),)),
    }


def reference(residual, queries, keys, values, video_ids, timestep, modulation, out_weight):
    mod_rows = modulation[timestep[0]]
    gate = mod_rows[0]
    shift = mod_rows[1]
    scale = mod_rows[2]
    factor = 1.0 / HEAD_DIM ** 0.5
    same = video_ids[:, None] == video_ids[None, :]
    q_heads = queries.reshape(TOKENS, HEADS, HEAD_DIM).transpose(1, 0, 2)
    k_heads = keys.reshape(TOKENS, HEADS, HEAD_DIM).transpose(1, 0, 2)
    v_heads = values.reshape(TOKENS, HEADS, HEAD_DIM).transpose(1, 0, 2)

    def one_head(items):
        q_one, k_one, v_one = items
        score = jnp.dot(q_one, k_one.T, preferred_element_type=jnp.float32) * factor
        score = jnp.where(same, score, -1e+30)
        top = lax.optimization_barrier(jnp.max(score, axis=1, keepdims=True))
        weight = jnp.where(same, jnp.exp(score - top), 0.0)
        total = lax.optimization_barrier(jnp.sum(weight, axis=1, keepdims=True))
        summed = jnp.dot(weight.astype(jnp.bfloat16), v_one, preferred_element_type=jnp.float32)
        return summed / total
    per_head = lax.map(one_head, (q_heads, k_heads, v_heads))
    attended = per_head.transpose(1, 0, 2).reshape(TOKENS, D).astype(jnp.bfloat16)
    projected = jnp.dot(attended, out_weight, preferred_element_type=jnp.float32)
    stream = residual.astype(jnp.float32) + gate[None, :] * projected
    row_sum = lax.optimization_barrier(jnp.sum(stream, axis=1, keepdims=True))
    row_sq = lax.optimization_barrier(jnp.sum(stream * stream, axis=1, keepdims=True))
    mean = row_sum / D
    var = row_sq / D - mean * mean
    normed = (stream - mean) * lax.rsqrt(var + 1e-06) * (1.0 + scale[None, :]) + shift[None, :]
    return (stream.astype(jnp.bfloat16), normed.astype(jnp.bfloat16))
```

```python
import functools
import math

import jax
import jax.numpy as jnp
from jax import lax
from jax.experimental import pallas as pl
from jax.experimental.pallas import tpu as pltpu
from jax.sharding import PartitionSpec as P

HEAD_DIM = 128
VIDEOS = 4
MESH = pl.DeviceIdType.MESH


def rows_at(index, count):
    return pl.ds(pl.multiple_of(index * count, count), count)


def whole(ref, sem):
    return pltpu.make_async_copy(ref, ref, sem)


def fused_kernel(
    n, mp_n, width,
    q_ref, k_ref, v_ref, ids_ref, mod_ref, res_ref, w_ref,
    hid_ref, mlp_ref,
    qkv, obuf, att, wbuf, res, acc, hid, mlp, counts, stat_mine, stat_other,
    qkv_send, qkv_recv, o_send, o_recv, fwd_send, fwd_recv,
    cnt_send, cnt_recv, stat_send, stat_recv, w_sem, res_sem, out_sem,
):
    seq_i = lax.axis_index("seq")
    mp_i = lax.axis_index("mp")
    me = seq_i * mp_n + mp_i
    rows = q_ref.shape[0]
    groups = qkv.shape[0]
    tokens = qkv.shape[2]
    columns = w_ref.shape[1]
    sibling = {"mp": 1 - mp_i}

    def device(p):
        return {"seq": lax.div(p, mp_n), "mp": lax.rem(p, mp_n)}

    def each_peer(body):
        def step(d, carry):
            body(lax.rem(me + d, n))
            return carry

        lax.fori_loop(1, n, step, 0)

    def load_weight(g, p):
        return pltpu.make_async_copy(
            w_ref.at[rows_at(p * groups + g, HEAD_DIM)],
            wbuf.at[g, rows_at(p, HEAD_DIM)],
            w_sem.at[g],
        )

    load_res = pltpu.make_async_copy(res_ref, res, res_sem)

    ids = ids_ref[...]
    below = [
        jnp.sum((ids <= k).astype(jnp.float32), axis=1, keepdims=True)
        for k in range(VIDEOS - 1)
    ]
    line = lax.broadcasted_iota(jnp.int32, (8, 128), 0)
    mine = jnp.where(line == 0, below[0], jnp.where(line == 1, below[1], below[2]))
    counts[rows_at(me, 8), :] = mine

    barrier = pltpu.get_barrier_semaphore()
    each_peer(
        lambda p: pl.semaphore_signal(
            barrier, inc=1, device_id=device(p), device_id_type=MESH
        )
    )
    pl.semaphore_wait(barrier, n - 1)

    def send_count(p):
        pltpu.make_async_remote_copy(
            src_ref=counts.at[rows_at(me, 8)],
            dst_ref=counts.at[rows_at(me, 8)],
            send_sem=cnt_send,
            recv_sem=cnt_recv,
            device_id=device(p),
            device_id_type=MESH,
        ).start()

    each_peer(send_count)

    def send_group(g):
        for t, ref in enumerate((k_ref, q_ref, v_ref)):

            def send(p, ref=ref, t=t):
                pltpu.make_async_remote_copy(
                    src_ref=ref.at[:, rows_at(p * groups + g, HEAD_DIM)],
                    dst_ref=qkv.at[g, t, rows_at(me, rows)],
                    send_sem=qkv_send.at[g],
                    recv_sem=qkv_recv.at[g],
                    device_id=device(p),
                    device_id_type=MESH,
                ).start()

            each_peer(send)
            pltpu.make_async_copy(
                ref.at[:, rows_at(me * groups + g, HEAD_DIM)],
                qkv.at[g, t, rows_at(me, rows)],
                qkv_recv.at[g],
            ).start()

    def attention(g, totals):
        lane = lax.broadcasted_iota(jnp.int32, (1, tokens), 1).astype(jnp.float32)
        key_ids = sum((lane >= c).astype(jnp.float32) for c in totals)
        tile = 2 * HEAD_DIM
        factor = math.log2(math.e) / HEAD_DIM**0.5

        def step(i, carry):
            at = rows_at(i, tile)
            place = (lax.broadcasted_iota(jnp.int32, (tile, 1), 0) + i * tile).astype(
                jnp.float32
            )
            own_ids = sum((place >= c).astype(jnp.float32) for c in totals)
            score = lax.dot_general(
                qkv[g, 1, at, :],
                qkv[g, 0],
                (((1,), (1,)), ((), ())),
                preferred_element_type=jnp.float32,
            )
            score = jnp.where(own_ids == key_ids, score, -1e30)
            top = jnp.max(score, axis=1, keepdims=True)
            weight = jnp.exp2((score - top) * factor)
            total = jnp.sum(weight, axis=1, keepdims=True)
            summed = jnp.dot(
                weight.astype(jnp.bfloat16),
                qkv[g, 2],
                preferred_element_type=jnp.float32,
            )
            obuf[g, at, :] = (summed / total).astype(jnp.bfloat16)
            return carry

        lax.fori_loop(0, tokens // tile, step, 0)

    def send_back(g):
        def send(p):
            pltpu.make_async_remote_copy(
                src_ref=obuf.at[g, rows_at(p, rows)],
                dst_ref=att.at[
                    g, rows_at(lax.rem(p, mp_n), rows), rows_at(me, HEAD_DIM)
                ],
                send_sem=o_send.at[g],
                recv_sem=o_recv.at[g],
                device_id=device(p),
                device_id_type=MESH,
            ).start()

        each_peer(send)
        pltpu.make_async_copy(
            obuf.at[g, rows_at(me, rows)],
            att.at[g, rows_at(mp_i, rows), rows_at(me, HEAD_DIM)],
            o_recv.at[g],
        ).start()

    def forward(g):
        half = att.at[g, rows_at(mp_i, rows)]
        return pltpu.make_async_remote_copy(
            src_ref=half,
            dst_ref=half,
            send_sem=fwd_send.at[g],
            recv_sem=fwd_recv.at[g],
            device_id=sibling,
            device_id_type=MESH,
        )

    def pass_on(g):
        whole(att.at[g, rows_at(mp_i, rows)], o_recv.at[g]).wait()
        forward(g).start()

    def project(g):
        whole(wbuf.at[g], w_sem.at[g]).wait()
        whole(att.at[g, rows_at(1 - mp_i, rows)], fwd_recv.at[g]).wait()
        tile = 2 * HEAD_DIM

        def step(i, carry):
            at = rows_at(i, tile)
            part = jnp.dot(
                att[g], wbuf[g, :, at], preferred_element_type=jnp.float32
            )
            acc[:, at] = part if g == 0 else acc[:, at] + part
            return carry

        lax.fori_loop(0, columns // tile, step, 0)

    send_group(0)
    if groups > 1:
        send_group(1)
    load_res.start()
    for g in range(groups):

        def start_load(p, carry, g=g):
            load_weight(g, p).start()
            return carry

        lax.fori_loop(0, n, start_load, 0)
    whole(counts.at[pl.ds(0, 8 * (n - 1))], cnt_recv).wait()
    sums = counts[pl.ds(0, 8), :]
    for r in range(1, n):
        sums = sums + counts[pl.ds(8 * r, 8), :]
    totals = [sums[k : k + 1, 0:1] for k in range(VIDEOS - 1)]

    for g in range(groups):
        whole(qkv.at[g], qkv_recv.at[g]).wait()
        if g + 2 < groups:
            send_group(g + 2)
        attention(g, totals)
        send_back(g)
        if g >= 1:
            pass_on(g - 1)
        if g >= 2:
            project(g - 2)
    if groups >= 2:
        project(groups - 2)
    pass_on(groups - 1)
    project(groups - 1)

    load_res.wait()
    gate = mod_ref[0:1, :]
    shift = mod_ref[1:2, :]
    scale = 1.0 + mod_ref[2:3, :]
    high = acc.shape[0]
    tile = 64
    side = lax.broadcasted_iota(jnp.int32, (tile, 128), 1) < 64

    def gated(i, carry):
        at = rows_at(i, tile)
        stream = res[at, :].astype(jnp.float32) + gate * acc[at, :]
        acc[at, :] = stream
        hid[at, :] = stream.astype(jnp.bfloat16)
        row_sum = jnp.sum(stream, axis=1, keepdims=True)
        row_sq = jnp.sum(stream * stream, axis=1, keepdims=True)
        stat_mine[at, :] = jnp.where(side, row_sum, row_sq)
        return carry

    lax.fori_loop(0, high // tile, gated, 0)
    stats = pltpu.make_async_remote_copy(
        src_ref=stat_mine,
        dst_ref=stat_other,
        send_sem=stat_send,
        recv_sem=stat_recv,
        device_id=sibling,
        device_id_type=MESH,
    )
    stats.start()
    store_hid = pltpu.make_async_copy(hid, hid_ref, out_sem.at[0])
    store_hid.start()
    stats.wait_recv()

    def normed(i, carry):
        at = rows_at(i, tile)
        both = stat_mine[at, :] + stat_other[at, :]
        mean = both[:, 0:1] / width
        var = both[:, 64:65] / width - mean * mean
        stream = acc[at, :]
        result = (stream - mean) * lax.rsqrt(var + 1e-06) * scale + shift
        mlp[at, :] = result.astype(jnp.bfloat16)
        return carry

    lax.fori_loop(0, high // tile, normed, 0)
    store_mlp = pltpu.make_async_copy(mlp, mlp_ref, out_sem.at[1])
    store_mlp.start()

    stats.wait_send()
    whole(counts.at[pl.ds(0, 8 * (n - 1))], cnt_send).wait()
    for g in range(groups):
        whole(qkv.at[g, :, pl.ds(0, rows * (n - 1))], qkv_send.at[g]).wait()
        whole(obuf.at[g, pl.ds(0, rows * (n - 1))], o_send.at[g]).wait()
        forward(g).wait_send()
    store_hid.wait()
    store_mlp.wait()


def fused(n, mp_n, residual, queries, keys, values, video_ids, timestep, modulation, out_weight):
    mod_rows = lax.dynamic_index_in_dim(modulation, timestep[0], 0, keepdims=False)
    rows, width = queries.shape
    high, columns = residual.shape
    tokens = rows * n
    groups = width // HEAD_DIM // n
    bf16 = jnp.bfloat16
    dma = pltpu.SemaphoreType.DMA
    anywhere = pl.BlockSpec(memory_space=pl.ANY)
    vmem = pl.BlockSpec(memory_space=pltpu.VMEM)
    out = jax.ShapeDtypeStruct(residual.shape, bf16)
    return pl.pallas_call(
        functools.partial(fused_kernel, n, mp_n, width),
        out_shape=(out, out),
        in_specs=[anywhere, anywhere, anywhere, vmem, vmem, anywhere, anywhere],
        out_specs=(anywhere, anywhere),
        scratch_shapes=[
            pltpu.VMEM((groups, 3, tokens, HEAD_DIM), bf16),
            pltpu.VMEM((groups, tokens, HEAD_DIM), bf16),
            pltpu.VMEM((groups, high, n * HEAD_DIM), bf16),
            pltpu.VMEM((groups, n * HEAD_DIM, columns), bf16),
            pltpu.VMEM((high, columns), bf16),
            pltpu.VMEM((high, columns), jnp.float32),
            pltpu.VMEM((high, columns), bf16),
            pltpu.VMEM((high, columns), bf16),
            pltpu.VMEM((8 * n, 128), jnp.float32),
            pltpu.VMEM((high, 128), jnp.float32),
            pltpu.VMEM((high, 128), jnp.float32),
            dma((groups,)), dma((groups,)), dma((groups,)), dma((groups,)),
            dma((groups,)), dma((groups,)),
            dma, dma, dma, dma, dma((groups,)), dma, dma((2,)),
        ],
        compiler_params=pltpu.CompilerParams(
            collective_id=0, has_side_effects=True, vmem_limit_bytes=52 * 2**20
        ),
    )(queries, keys, values, video_ids.reshape(1, rows), mod_rows, residual, out_weight)


def attend(carry, q_rows, q_ids, key_rows, value_rows, key_ids):
    top, total, summed = carry
    rows = q_rows.shape[0]
    count = key_rows.shape[0]
    heads = q_rows.shape[1] // HEAD_DIM
    factor = 1.0 / HEAD_DIM**0.5
    q_heads = q_rows.reshape(rows, heads, HEAD_DIM)
    k_heads = key_rows.reshape(count, heads, HEAD_DIM)
    v_heads = value_rows.reshape(count, heads, HEAD_DIM)
    same = (q_ids[:, None] == key_ids[None, :])[None]
    new_top, new_total, new_summed = ([], [], [])
    for first in range(0, heads, 3):
        score = (
            jnp.einsum(
                "thd,nhd->htn",
                q_heads[:, first : first + 3],
                k_heads[:, first : first + 3],
                preferred_element_type=jnp.float32,
            )
            * factor
        )
        score = jnp.where(same, score, -1e30)
        old_top = top[first : first + 3]
        peak = jnp.maximum(old_top, jnp.max(score, axis=2))
        weight = jnp.where(same, jnp.exp(score - peak[:, :, None]), 0.0)
        new_top.append(peak)
        new_total.append(jnp.sum(weight, axis=2))
        part_sum = jnp.einsum(
            "htn,nhd->htd",
            weight.astype(jnp.bfloat16),
            v_heads[:, first : first + 3],
            preferred_element_type=jnp.float32,
        )
        new_summed.append(part_sum)
    return (
        jnp.concatenate(new_top, 0),
        jnp.concatenate(new_total, 0),
        jnp.concatenate(new_summed, 0),
    )


def attend_maybe(carry, q_rows, q_ids, key_rows, value_rows, key_ids):
    return attend(carry, q_rows, q_ids, key_rows, value_rows, key_ids)


def start_state(q_rows):
    rows = q_rows.shape[0]
    heads = q_rows.shape[1] // HEAD_DIM
    return (
        jnp.full((heads, rows), -1e30, jnp.float32),
        jnp.zeros((heads, rows), jnp.float32),
        jnp.zeros((heads, rows, HEAD_DIM), jnp.float32),
    )


def finish(state, q_rows):
    top, total, summed = state
    rows = q_rows.shape[0]
    heads = q_rows.shape[1] // HEAD_DIM
    result = summed / total[:, :, None]
    return result.transpose(1, 0, 2).reshape(rows, heads * HEAD_DIM).astype(jnp.bfloat16)


def local(residual, queries, keys, values, video_ids, timestep, modulation, out_weight):
    steps_count = modulation.shape[0]
    picker = (jnp.arange(steps_count, dtype=jnp.int32) == timestep[0]).astype(jnp.float32)
    mod_rows = jnp.einsum("s,scd->cd", picker, modulation, precision=lax.Precision.HIGHEST)
    gate = mod_rows[0]
    shift = mod_rows[1]
    scale = mod_rows[2]
    width = queries.shape[1]
    state = attend_maybe(
        start_state(queries),
        queries,
        video_ids,
        lax.all_gather(keys, ("seq", "mp"), axis=0, tiled=True),
        lax.all_gather(values, ("seq", "mp"), axis=0, tiled=True),
        lax.all_gather(video_ids, ("seq", "mp"), axis=0, tiled=True),
    )
    attended = finish(state, queries)
    projected = jnp.dot(
        lax.all_gather(attended, "mp", axis=0, tiled=True),
        out_weight,
        preferred_element_type=jnp.float32,
    )
    stream = residual.astype(jnp.float32) + gate[None, :] * projected
    row_sum = jnp.sum(stream, axis=1, keepdims=True)
    row_sq = jnp.sum(stream * stream, axis=1, keepdims=True)
    row_sum, row_sq = lax.psum((row_sum, row_sq), "mp")
    mean = row_sum / width
    var = row_sq / width - mean * mean
    normed = (stream - mean) * lax.rsqrt(var + 1e-06) * (1.0 + scale[None, :]) + shift[None, :]
    return (stream.astype(jnp.bfloat16), normed.astype(jnp.bfloat16))


def choose(mesh):
    seq_n, mp_n = mesh.shape["seq"], mesh.shape["mp"]
    n = seq_n * mp_n

    def run(*arrays):
        queries = arrays[1]
        rows, width = queries.shape
        if mp_n == 2 and width // HEAD_DIM % n == 0 and rows % 64 == 0 and rows * n % 256 == 0:
            return fused(n, mp_n, *arrays)
        return local(*arrays)

    return run


def solution(mesh):
    return jax.shard_map(
        choose(mesh),
        mesh=mesh,
        in_specs=(
            P(("dp", "seq"), "mp"),
            P(("dp", "seq", "mp"), None),
            P(("dp", "seq", "mp"), None),
            P(("dp", "seq", "mp"), None),
            P(("dp", "seq", "mp")),
            P("dp"),
            P(None, None, "mp"),
            P(None, "mp"),
        ),
        out_specs=(P(("dp", "seq"), "mp"), P(("dp", "seq"), "mp")),
        check_vma=False,
    )
```

```python
import functools
import math

import jax
import jax.numpy as jnp
from jax import lax
from jax.experimental import pallas as pl
from jax.experimental.pallas import tpu as pltpu
from jax.sharding import PartitionSpec as P

HEAD_DIM = 128
VIDEOS = 4
MESH = pl.DeviceIdType.MESH


def rows_at(index, count):
    return pl.ds(pl.multiple_of(index * count, count), count)


def whole(ref, sem):
    return pltpu.make_async_copy(ref, ref, sem)


def fused_kernel(
    n, mp_n,
    q_ref, k_ref, v_ref, ids_ref, step_ref, mod_ref, res_ref, w_ref,
    acc, stat_out, mod_out,
    stage, qkv, weights, weight_sum, obuf, att, wbuf, res, mods, ids_mine, counts,
    stat_mine, stat_other,
    stage_sem, qkv_send, kq_recv, v_recv, o_send, o_recv, fwd_send, fwd_recv,
    cnt_send, cnt_recv, stat_send, stat_recv, w_sem, in_sem,
):
    seq_i = lax.axis_index("seq")
    mp_i = lax.axis_index("mp")
    me = seq_i * mp_n + mp_i
    rows = q_ref.shape[0]
    groups = qkv.shape[0]
    tokens = qkv.shape[2]
    columns = w_ref.shape[1]
    sibling = {"mp": 1 - mp_i}

    def device(p):
        return {"seq": lax.div(p, mp_n), "mp": lax.rem(p, mp_n)}

    def each_peer(body):
        def step(d, carry):
            body(lax.rem(me + d, n))
            return carry

        lax.fori_loop(1, n, step, 0)

    def every(body):
        def step(p, carry):
            body(p)
            return carry

        lax.fori_loop(0, n, step, 0)

    sources = (k_ref, q_ref, v_ref)
    slots = ((0, 1), (2,))

    def part_recv(g, part):
        return (kq_recv, v_recv)[part].at[g]

    def load_part(g, part):
        for t in slots[part]:

            def load(p, t=t):
                pltpu.make_async_copy(
                    sources[t].at[:, rows_at(p * groups + g, HEAD_DIM)],
                    stage.at[g, t, p],
                    stage_sem.at[g, part],
                ).start()

            every(load)
            pltpu.make_async_copy(
                sources[t].at[:, rows_at(me * groups + g, HEAD_DIM)],
                qkv.at[g, t, rows_at(me, rows)],
                part_recv(g, part),
            ).start()

    def part_of(ref, g, part):
        return ref.at[g, pl.ds(slots[part][0], len(slots[part]))]

    def send_part(g, part):
        whole(part_of(stage, g, part), stage_sem.at[g, part]).wait()
        for t in slots[part]:

            def send(p, t=t):
                pltpu.make_async_remote_copy(
                    src_ref=stage.at[g, t, p],
                    dst_ref=qkv.at[g, t, rows_at(me, rows)],
                    send_sem=qkv_send.at[g, part],
                    recv_sem=part_recv(g, part),
                    device_id=device(p),
                    device_id_type=MESH,
                ).start()

            each_peer(send)

    def wait_part(g, part):
        whole(part_of(qkv, g, part), part_recv(g, part)).wait()

    barrier = pltpu.get_barrier_semaphore()
    each_peer(
        lambda p: pl.semaphore_signal(
            barrier, inc=1, device_id=device(p), device_id_type=MESH
        )
    )
    load_part(0, 0)
    load_part(0, 1)
    load_ids = pltpu.make_async_copy(ids_ref, ids_mine, in_sem.at[0])
    load_res = pltpu.make_async_copy(res_ref, res, in_sem.at[1])
    load_mods = pltpu.make_async_copy(mod_ref, mods, in_sem.at[2])
    load_ids.start()
    for g in range(1, groups):
        load_part(g, 0)
        load_part(g, 1)
    pl.semaphore_wait(barrier, n - 1)

    order = [(g, part) for g in range(groups) for part in range(2)]
    ahead = 3
    for g, part in order[:ahead]:
        send_part(g, part)

    load_ids.wait()
    ids = ids_mine[...]
    below = [
        jnp.sum((ids <= k).astype(jnp.float32), axis=1, keepdims=True)
        for k in range(VIDEOS - 1)
    ]
    line = lax.broadcasted_iota(jnp.int32, (8, 128), 0)
    mine = jnp.where(line == 0, below[0], jnp.where(line == 1, below[1], below[2]))
    counts[rows_at(me, 8), :] = mine

    def send_count(p):
        pltpu.make_async_remote_copy(
            src_ref=counts.at[rows_at(me, 8)],
            dst_ref=counts.at[rows_at(me, 8)],
            send_sem=cnt_send,
            recv_sem=cnt_recv,
            device_id=device(p),
            device_id_type=MESH,
        ).start()

    each_peer(send_count)
    load_res.start()
    load_mods.start()
    for g in range(groups):

        def load_weight(p, g=g):
            pltpu.make_async_copy(
                w_ref.at[rows_at(p * groups + g, HEAD_DIM)],
                wbuf.at[g, rows_at(p, HEAD_DIM)],
                w_sem.at[g],
            ).start()

        every(load_weight)

    whole(counts.at[pl.ds(0, 8 * (n - 1))], cnt_recv).wait()
    sums = counts[pl.ds(0, 8), :]
    for r in range(1, n):
        sums = sums + counts[pl.ds(8 * r, 8), :]
    totals = [sums[k : k + 1, 0:1] for k in range(VIDEOS - 1)]
    factor = math.log2(math.e) / HEAD_DIM**0.5

    def scores(g):
        lane = lax.broadcasted_iota(jnp.int32, (1, tokens), 1).astype(jnp.float32)
        key_ids = sum((lane >= c).astype(jnp.float32) for c in totals)

        def step(p):
            at = rows_at(p, rows)
            place = (lax.broadcasted_iota(jnp.int32, (rows, 1), 0) + p * rows).astype(
                jnp.float32
            )
            own_ids = sum((place >= c).astype(jnp.float32) for c in totals)
            score = lax.dot_general(
                qkv[g, 1, at, :],
                qkv[g, 0],
                (((1,), (1,)), ((), ())),
                preferred_element_type=jnp.float32,
            )
            score = jnp.where(own_ids == key_ids, score, -1e30)
            top = jnp.max(score, axis=1, keepdims=True)
            weight = jnp.exp2((score - top) * factor)
            total = jnp.sum(weight, axis=1, keepdims=True)
            weights[at, :] = weight.astype(jnp.bfloat16)
            weight_sum[at, :] = jnp.broadcast_to(total, (rows, HEAD_DIM))

        every(step)

    def attend_rows(g, p):
        at = rows_at(p, rows)
        summed = jnp.dot(
            weights[at, :], qkv[g, 2], preferred_element_type=jnp.float32
        )
        obuf[g, at, :] = (summed / weight_sum[at, :]).astype(jnp.bfloat16)

    def attend_and_send(g):
        def send(p):
            attend_rows(g, p)
            pltpu.make_async_remote_copy(
                src_ref=obuf.at[g, rows_at(p, rows)],
                dst_ref=att.at[
                    g, rows_at(lax.rem(p, mp_n), rows), rows_at(me, HEAD_DIM)
                ],
                send_sem=o_send.at[g],
                recv_sem=o_recv.at[g, me],
                device_id=device(p),
                device_id_type=MESH,
            ).start()

        each_peer(send)
        attend_rows(g, me)
        pltpu.make_async_copy(
            obuf.at[g, rows_at(me, rows)],
            att.at[g, rows_at(mp_i, rows), rows_at(me, HEAD_DIM)],
            o_recv.at[g, me],
        ).start()

    def pass_on(g):
        def step(d, carry):
            p = lax.rem(me + n - d, n)
            block = att.at[g, rows_at(mp_i, rows), rows_at(p, HEAD_DIM)]
            whole(block, o_recv.at[g, p]).wait()
            pltpu.make_async_remote_copy(
                src_ref=block,
                dst_ref=block,
                send_sem=fwd_send.at[g],
                recv_sem=fwd_recv.at[g],
                device_id=sibling,
                device_id_type=MESH,
            ).start()
            return carry

        lax.fori_loop(1, n + 1, step, 0)

    def project(g, half):
        rows_of = rows_at(half, rows)
        tile = 2 * HEAD_DIM

        def step(i, carry):
            at = rows_at(i, tile)
            part = jnp.dot(
                att[g, rows_of, :], wbuf[g, :, at], preferred_element_type=jnp.float32
            )
            acc[rows_of, at] = part if g == 0 else acc[rows_of, at] + part
            return carry

        lax.fori_loop(0, columns // tile, step, 0)

    def wait_forward(g):
        whole(att.at[g, rows_at(1 - mp_i, rows)], fwd_recv.at[g]).wait()

    def project_both(g):
        whole(wbuf.at[g], w_sem.at[g]).wait()
        wait_forward(g)
        project(g, mp_i)
        project(g, 1 - mp_i)

    for g in range(groups):
        for part in range(2):
            wait_part(g, part)
            later = 2 * g + part + ahead
            if later < len(order):
                send_part(*order[later])
            if part == 0:
                scores(g)
        attend_and_send(g)
        if g >= 1:
            pass_on(g - 1)
        if g >= 2:
            project_both(g - 2)
    if groups >= 2:
        project_both(groups - 2)
    last = groups - 1
    pass_on(last)

    load_res.wait()
    load_mods.wait()
    chosen = step_ref[0]
    gate = mods[0, pl.ds(chosen, 1), :]
    mod_out[0:1, :] = mods[1, pl.ds(chosen, 1), :]
    mod_out[1:2, :] = mods[2, pl.ds(chosen, 1), :]
    tile = rows // 3 if rows % 48 == 0 else 16
    side = lax.broadcasted_iota(jnp.int32, (tile, 128), 1) < 64

    def stats(half):
        part = rows_at(half, rows)
        return pltpu.make_async_remote_copy(
            src_ref=stat_mine.at[part],
            dst_ref=stat_other.at[part],
            send_sem=stat_send.at[half],
            recv_sem=stat_recv.at[half],
            device_id=sibling,
            device_id_type=MESH,
        )

    def finish(half):
        project(last, half)

        def gated(i, carry):
            at = rows_at(half * (rows // tile) + i, tile)
            stream = res[at, :].astype(jnp.float32) + gate * acc[at, :]
            acc[at, :] = stream
            row_sum = jnp.sum(stream, axis=1, keepdims=True)
            row_sq = jnp.sum(stream * stream, axis=1, keepdims=True)
            stat_mine[at, :] = jnp.where(side, row_sum, row_sq)
            return carry

        lax.fori_loop(0, rows // tile, gated, 0)
        stats(half).start()

    whole(wbuf.at[last], w_sem.at[last]).wait()
    finish(mp_i)
    wait_forward(last)
    finish(1 - mp_i)

    whole(counts.at[pl.ds(0, 8 * (n - 1))], cnt_send).wait()
    for g in range(groups):
        for part in range(2):
            sent = part_of(qkv, g, part).at[:, pl.ds(0, rows * (n - 1))]
            whole(sent, qkv_send.at[g, part]).wait()
        whole(obuf.at[g, pl.ds(0, rows * (n - 1))], o_send.at[g]).wait()
        whole(att.at[g, rows_at(mp_i, rows)], fwd_send.at[g]).wait()
    for half in range(2):
        stats(half).wait_recv()
    stat_out[...] = stat_mine[...] + stat_other[...]
    for half in range(2):
        stats(half).wait_send()


def fused(n, mp_n, residual, queries, keys, values, video_ids, timestep, modulation, out_weight):
    rows, width = queries.shape
    high, columns = residual.shape
    tokens = rows * n
    groups = width // HEAD_DIM // n
    steps = modulation.shape[0]
    bf16, f32 = jnp.bfloat16, jnp.float32
    dma = pltpu.SemaphoreType.DMA
    anywhere = pl.BlockSpec(memory_space=pl.ANY)
    smem = pl.BlockSpec(memory_space=pltpu.SMEM)
    vmem = pl.BlockSpec(memory_space=pltpu.VMEM)
    stream, stat, mods = pl.pallas_call(
        functools.partial(fused_kernel, n, mp_n),
        out_shape=(
            jax.ShapeDtypeStruct((high, columns), f32),
            jax.ShapeDtypeStruct((high, 128), f32),
            jax.ShapeDtypeStruct((2, columns), f32),
        ),
        in_specs=[anywhere, anywhere, anywhere, anywhere, smem, anywhere, anywhere, anywhere],
        out_specs=(vmem, vmem, vmem),
        scratch_shapes=[
            pltpu.VMEM((groups, 3, n, rows, HEAD_DIM), bf16),
            pltpu.VMEM((groups, 3, tokens, HEAD_DIM), bf16),
            pltpu.VMEM((tokens, tokens), bf16),
            pltpu.VMEM((tokens, HEAD_DIM), f32),
            pltpu.VMEM((groups, tokens, HEAD_DIM), bf16),
            pltpu.VMEM((groups, high, n * HEAD_DIM), bf16),
            pltpu.VMEM((groups, n * HEAD_DIM, columns), bf16),
            pltpu.VMEM((high, columns), bf16),
            pltpu.VMEM((3, steps, columns), f32),
            pltpu.VMEM((1, rows), jnp.int32),
            pltpu.VMEM((8 * n, 128), f32),
            pltpu.VMEM((high, 128), f32),
            pltpu.VMEM((high, 128), f32),
            dma((groups, 2)), dma((groups, 2)), dma((groups,)), dma((groups,)),
            dma((groups,)), dma((groups, n)), dma((groups,)), dma((groups,)),
            dma, dma, dma((2,)), dma((2,)), dma((groups,)), dma((3,)),
        ],
        compiler_params=pltpu.CompilerParams(
            collective_id=0, has_side_effects=True, vmem_limit_bytes=52 * 2**20
        ),
    )(
        queries, keys, values, video_ids.reshape(1, rows), timestep,
        modulation.transpose(1, 0, 2), residual, out_weight,
    )
    mean = stat[:, 0:1] / width
    var = stat[:, 64:65] / width - mean * mean
    normed = (stream - mean) * lax.rsqrt(var + 1e-06) * (1.0 + mods[1:2]) + mods[0:1]
    return (stream.astype(bf16), normed.astype(bf16))


def attend(carry, q_rows, q_ids, key_rows, value_rows, key_ids):
    top, total, summed = carry
    rows = q_rows.shape[0]
    count = key_rows.shape[0]
    heads = q_rows.shape[1] // HEAD_DIM
    factor = 1.0 / HEAD_DIM**0.5
    q_heads = q_rows.reshape(rows, heads, HEAD_DIM)
    k_heads = key_rows.reshape(count, heads, HEAD_DIM)
    v_heads = value_rows.reshape(count, heads, HEAD_DIM)
    same = (q_ids[:, None] == key_ids[None, :])[None]
    new_top, new_total, new_summed = ([], [], [])
    for first in range(0, heads, 3):
        score = (
            jnp.einsum(
                "thd,nhd->htn",
                q_heads[:, first : first + 3],
                k_heads[:, first : first + 3],
                preferred_element_type=jnp.float32,
            )
            * factor
        )
        score = jnp.where(same, score, -1e30)
        old_top = top[first : first + 3]
        peak = jnp.maximum(old_top, jnp.max(score, axis=2))
        weight = jnp.where(same, jnp.exp(score - peak[:, :, None]), 0.0)
        new_top.append(peak)
        new_total.append(jnp.sum(weight, axis=2))
        part_sum = jnp.einsum(
            "htn,nhd->htd",
            weight.astype(jnp.bfloat16),
            v_heads[:, first : first + 3],
            preferred_element_type=jnp.float32,
        )
        new_summed.append(part_sum)
    return (
        jnp.concatenate(new_top, 0),
        jnp.concatenate(new_total, 0),
        jnp.concatenate(new_summed, 0),
    )


def attend_maybe(carry, q_rows, q_ids, key_rows, value_rows, key_ids):
    return attend(carry, q_rows, q_ids, key_rows, value_rows, key_ids)


def start_state(q_rows):
    rows = q_rows.shape[0]
    heads = q_rows.shape[1] // HEAD_DIM
    return (
        jnp.full((heads, rows), -1e30, jnp.float32),
        jnp.zeros((heads, rows), jnp.float32),
        jnp.zeros((heads, rows, HEAD_DIM), jnp.float32),
    )


def finish(state, q_rows):
    top, total, summed = state
    rows = q_rows.shape[0]
    heads = q_rows.shape[1] // HEAD_DIM
    result = summed / total[:, :, None]
    return result.transpose(1, 0, 2).reshape(rows, heads * HEAD_DIM).astype(jnp.bfloat16)


def local(residual, queries, keys, values, video_ids, timestep, modulation, out_weight):
    steps_count = modulation.shape[0]
    picker = (jnp.arange(steps_count, dtype=jnp.int32) == timestep[0]).astype(jnp.float32)
    mod_rows = jnp.einsum("s,scd->cd", picker, modulation, precision=lax.Precision.HIGHEST)
    gate = mod_rows[0]
    shift = mod_rows[1]
    scale = mod_rows[2]
    width = queries.shape[1]
    state = attend_maybe(
        start_state(queries),
        queries,
        video_ids,
        lax.all_gather(keys, ("seq", "mp"), axis=0, tiled=True),
        lax.all_gather(values, ("seq", "mp"), axis=0, tiled=True),
        lax.all_gather(video_ids, ("seq", "mp"), axis=0, tiled=True),
    )
    attended = finish(state, queries)
    projected = jnp.dot(
        lax.all_gather(attended, "mp", axis=0, tiled=True),
        out_weight,
        preferred_element_type=jnp.float32,
    )
    stream = residual.astype(jnp.float32) + gate[None, :] * projected
    row_sum = jnp.sum(stream, axis=1, keepdims=True)
    row_sq = jnp.sum(stream * stream, axis=1, keepdims=True)
    row_sum, row_sq = lax.psum((row_sum, row_sq), "mp")
    mean = row_sum / width
    var = row_sq / width - mean * mean
    normed = (stream - mean) * lax.rsqrt(var + 1e-06) * (1.0 + scale[None, :]) + shift[None, :]
    return (stream.astype(jnp.bfloat16), normed.astype(jnp.bfloat16))


def choose(mesh):
    seq_n, mp_n = mesh.shape["seq"], mesh.shape["mp"]
    n = seq_n * mp_n

    def run(*arrays):
        queries = arrays[1]
        rows, width = queries.shape
        if mp_n == 2 and width // HEAD_DIM % n == 0 and rows % 64 == 0 and rows * n % 256 == 0:
            return fused(n, mp_n, *arrays)
        return local(*arrays)

    return run


def solution(mesh):
    return jax.shard_map(
        choose(mesh),
        mesh=mesh,
        in_specs=(
            P(("dp", "seq"), "mp"),
            P(("dp", "seq", "mp"), None),
            P(("dp", "seq", "mp"), None),
            P(("dp", "seq", "mp"), None),
            P(("dp", "seq", "mp")),
            P("dp"),
            P(None, None, "mp"),
            P(None, "mp"),
        ),
        out_specs=(P(("dp", "seq"), "mp"), P(("dp", "seq"), "mp")),
        check_vma=False,
    )
```

```python
import functools

import jax
import jax.numpy as jnp
from jax import lax
from jax.experimental import pallas as pl
from jax.experimental.pallas import tpu as pltpu
from jax.sharding import PartitionSpec as P

HEAD_DIM = 128
VIDEOS = 4
MARK = 2.0**50
MESH = pl.DeviceIdType.MESH


def rows_at(index, count):
    return pl.ds(pl.multiple_of(index * count, count), count)


def whole(ref, sem):
    return pltpu.make_async_copy(ref, ref, sem)


def fused_kernel(
    n, mp_n,
    q_ref, k_ref, v_ref, ids_ref, step_ref, mod_ref, res_ref, w_ref,
    stream_ref, stat_out, mod_out,
    acc, stage, qkv, key_marks, query_marks, values_t, obuf, att, wbuf, res, mods, ids_mine, counts,
    stat_mine, stat_other,
    stage_sem, qkv_send, kq_recv, v_recv, o_send, o_recv, fwd_send, fwd_recv,
    cnt_send, cnt_recv, stat_send, stat_recv, w_sem, in_sem, out_sem,
):
    seq_i = lax.axis_index("seq")
    mp_i = lax.axis_index("mp")
    me = seq_i * mp_n + mp_i
    rows = q_ref.shape[0]
    groups = qkv.shape[0]
    tokens = qkv.shape[2]
    columns = w_ref.shape[1]
    sibling = {"mp": 1 - mp_i}

    def device(p):
        return {"seq": lax.div(p, mp_n), "mp": lax.rem(p, mp_n)}

    def each_peer(body):
        def step(d, carry):
            body(lax.rem(me + d, n))
            return carry

        lax.fori_loop(1, n, step, 0)

    def every(body):
        def step(p, carry):
            body(p)
            return carry

        lax.fori_loop(0, n, step, 0)

    sources = (k_ref, q_ref, v_ref)
    slots = ((0, 1), (2,))

    def part_recv(g, part):
        return (kq_recv, v_recv)[part].at[g]

    def load_part(g, part):
        for t in slots[part]:

            def load(p, t=t):
                pltpu.make_async_copy(
                    sources[t].at[:, rows_at(p * groups + g, HEAD_DIM)],
                    stage.at[g, t, p],
                    stage_sem.at[g, part],
                ).start()

            every(load)
            pltpu.make_async_copy(
                sources[t].at[:, rows_at(me * groups + g, HEAD_DIM)],
                qkv.at[g, t, rows_at(me, rows)],
                part_recv(g, part),
            ).start()

    def part_of(ref, g, part):
        return ref.at[g, pl.ds(slots[part][0], len(slots[part]))]

    def send_part(g, part):
        whole(part_of(stage, g, part), stage_sem.at[g, part]).wait()
        for t in slots[part]:

            def send(p, t=t):
                pltpu.make_async_remote_copy(
                    src_ref=stage.at[g, t, p],
                    dst_ref=qkv.at[g, t, rows_at(me, rows)],
                    send_sem=qkv_send.at[g, part],
                    recv_sem=part_recv(g, part),
                    device_id=device(p),
                    device_id_type=MESH,
                ).start()

            each_peer(send)

    def wait_part(g, part):
        whole(part_of(qkv, g, part), part_recv(g, part)).wait()

    barrier = pltpu.get_barrier_semaphore()
    each_peer(
        lambda p: pl.semaphore_signal(
            barrier, inc=1, device_id=device(p), device_id_type=MESH
        )
    )
    load_part(0, 0)
    load_part(0, 1)
    load_ids = pltpu.make_async_copy(ids_ref, ids_mine, in_sem.at[0])
    load_res = pltpu.make_async_copy(res_ref, res, in_sem.at[1])
    load_mods = pltpu.make_async_copy(mod_ref, mods, in_sem.at[2])
    load_ids.start()
    for g in range(1, groups):
        load_part(g, 0)
        load_part(g, 1)
    pl.semaphore_wait(barrier, n - 1)

    order = [(g, part) for g in range(groups) for part in range(2)]
    ahead = 3
    for g, part in order[:ahead]:
        send_part(g, part)

    load_ids.wait()
    ids = ids_mine[...]
    below = [
        jnp.sum((ids <= k).astype(jnp.float32), axis=1, keepdims=True)
        for k in range(VIDEOS - 1)
    ]
    line = lax.broadcasted_iota(jnp.int32, (8, 128), 0)
    mine = jnp.where(line == 0, below[0], jnp.where(line == 1, below[1], below[2]))
    counts[rows_at(me, 8), :] = mine

    def send_count(p):
        pltpu.make_async_remote_copy(
            src_ref=counts.at[rows_at(me, 8)],
            dst_ref=counts.at[rows_at(me, 8)],
            send_sem=cnt_send,
            recv_sem=cnt_recv,
            device_id=device(p),
            device_id_type=MESH,
        ).start()

    each_peer(send_count)
    load_res.start()
    load_mods.start()
    for g in range(groups):

        def load_weight(p, g=g):
            pltpu.make_async_copy(
                w_ref.at[rows_at(p * groups + g, HEAD_DIM)],
                wbuf.at[g, rows_at(p, HEAD_DIM)],
                w_sem.at[g],
            ).start()

        every(load_weight)

    whole(counts.at[pl.ds(0, 8 * (n - 1))], cnt_recv).wait()
    sums = counts[pl.ds(0, 8), :]
    for r in range(1, n):
        sums = sums + counts[pl.ds(8 * r, 8), :]
    totals = [sums[k : k + 1, 0:1] for k in range(VIDEOS - 1)]
    tile = 2 * HEAD_DIM

    def mark(i, carry):
        at = rows_at(i, tile)
        place = (lax.broadcasted_iota(jnp.int32, (tile, 1), 0) + i * tile).astype(
            jnp.float32
        )
        own = sum((place >= c).astype(jnp.float32) for c in totals)
        video = lax.broadcasted_iota(jnp.int32, (tile, HEAD_DIM), 1).astype(jnp.float32)
        key_marks[at, :] = jnp.where(own == video, -MARK, 0.0).astype(jnp.bfloat16)
        other = jnp.where(own == video, 0.0, MARK)
        query_marks[at, :] = jnp.where(video < VIDEOS, other, 0.0).astype(jnp.bfloat16)
        return carry

    lax.fori_loop(0, tokens // tile, mark, 0)
    values_t[HEAD_DIM:, :] = jnp.ones((values_t.shape[0] - HEAD_DIM, tokens), jnp.bfloat16)
    chunk = tokens // 2
    peers = n // 2

    def attend_tile(g, start):
        at = pl.ds(pl.multiple_of(start, tile), tile)
        score = lax.dot_general(
            jnp.concatenate([qkv[g, 0], key_marks[...]], axis=1),
            jnp.concatenate([qkv[g, 1, at, :], query_marks[at, :]], axis=1),
            (((1,), (1,)), ((), ())),
            preferred_element_type=jnp.float32,
        )
        top = jnp.max(score, axis=0, keepdims=True)
        weight = jnp.exp((score - top) * (1.0 / HEAD_DIM**0.5)).astype(jnp.bfloat16)
        summed = jnp.dot(values_t[...], weight, preferred_element_type=jnp.float32)
        result = summed[:HEAD_DIM] / summed[HEAD_DIM : HEAD_DIM + 1]
        obuf[g, at, :] = result.T.astype(jnp.bfloat16)

    def attend_and_send(g):
        values_t[:HEAD_DIM, :] = qkv[g, 2].T

        def half(j, carry):
            part = lax.rem(lax.div(me, peers) + 1 + j, 2)
            for i in range(chunk // tile):
                attend_tile(g, part * chunk + i * tile)

            def send(d, carry):
                p = part * peers + lax.rem(me + d, peers)
                block = obuf.at[g, rows_at(p, rows)]
                there = att.at[
                    g, rows_at(lax.rem(p, mp_n), rows), rows_at(me, HEAD_DIM)
                ]

                @pl.when(p != me)
                def _():
                    pltpu.make_async_remote_copy(
                        src_ref=block,
                        dst_ref=there,
                        send_sem=o_send.at[g],
                        recv_sem=o_recv.at[g, me],
                        device_id=device(p),
                        device_id_type=MESH,
                    ).start()

                @pl.when(p == me)
                def _():
                    pltpu.make_async_copy(block, there, o_recv.at[g, me]).start()

                return carry

            return lax.fori_loop(0, peers, send, carry)

        lax.fori_loop(0, 2, half, 0)

    def pass_on(g):
        def step(d, carry):
            p = lax.rem(me + n - d, n)
            block = att.at[g, rows_at(mp_i, rows), rows_at(p, HEAD_DIM)]
            whole(block, o_recv.at[g, p]).wait()
            pltpu.make_async_remote_copy(
                src_ref=block,
                dst_ref=block,
                send_sem=fwd_send.at[g],
                recv_sem=fwd_recv.at[g],
                device_id=sibling,
                device_id_type=MESH,
            ).start()
            return carry

        lax.fori_loop(1, n + 1, step, 0)

    def project(g, half):
        rows_of = rows_at(half, rows)
        tile = 2 * HEAD_DIM

        def step(i, carry):
            at = rows_at(i, tile)
            part = jnp.dot(
                att[g, rows_of, :], wbuf[g, :, at], preferred_element_type=jnp.float32
            )
            acc[rows_of, at] = part if g == 0 else acc[rows_of, at] + part
            return carry

        lax.fori_loop(0, columns // tile, step, 0)

    def wait_forward(g):
        whole(att.at[g, rows_at(1 - mp_i, rows)], fwd_recv.at[g]).wait()

    def project_both(g):
        whole(wbuf.at[g], w_sem.at[g]).wait()
        wait_forward(g)
        project(g, mp_i)
        project(g, 1 - mp_i)

    for g in range(groups):
        for part in range(2):
            wait_part(g, part)
            later = 2 * g + part + ahead
            if later < len(order):
                send_part(*order[later])
        attend_and_send(g)
        if g >= 1:
            pass_on(g - 1)
        if g >= 2:
            project_both(g - 2)
    if groups >= 2:
        project_both(groups - 2)
    last = groups - 1
    pass_on(last)

    load_res.wait()
    load_mods.wait()
    chosen = step_ref[0]
    gate = mods[0, pl.ds(chosen, 1), :]
    mod_out[0:1, :] = mods[1, pl.ds(chosen, 1), :]
    mod_out[1:2, :] = mods[2, pl.ds(chosen, 1), :]
    tile = rows // 3 if rows % 48 == 0 else 16
    side = lax.broadcasted_iota(jnp.int32, (tile, 128), 1) < 64

    def stats(half):
        part = rows_at(half, rows)
        return pltpu.make_async_remote_copy(
            src_ref=stat_mine.at[part],
            dst_ref=stat_other.at[part],
            send_sem=stat_send.at[half],
            recv_sem=stat_recv.at[half],
            device_id=sibling,
            device_id_type=MESH,
        )

    def store(half):
        part = rows_at(half, rows)
        return pltpu.make_async_copy(acc.at[part], stream_ref.at[part], out_sem.at[half])

    def finish(half):
        project(last, half)

        def gated(i, carry):
            at = rows_at(half * (rows // tile) + i, tile)
            stream = res[at, :].astype(jnp.float32) + gate * acc[at, :]
            acc[at, :] = stream
            row_sum = jnp.sum(stream, axis=1, keepdims=True)
            row_sq = jnp.sum(stream * stream, axis=1, keepdims=True)
            stat_mine[at, :] = jnp.where(side, row_sum, row_sq)
            return carry

        lax.fori_loop(0, rows // tile, gated, 0)
        stats(half).start()
        store(half).start()

    whole(wbuf.at[last], w_sem.at[last]).wait()
    finish(mp_i)
    wait_forward(last)
    finish(1 - mp_i)

    whole(counts.at[pl.ds(0, 8 * (n - 1))], cnt_send).wait()
    for g in range(groups):
        for part in range(2):
            sent = part_of(qkv, g, part).at[:, pl.ds(0, rows * (n - 1))]
            whole(sent, qkv_send.at[g, part]).wait()
        whole(obuf.at[g, pl.ds(0, rows * (n - 1))], o_send.at[g]).wait()
        whole(att.at[g, rows_at(mp_i, rows)], fwd_send.at[g]).wait()
    for half in range(2):
        stats(half).wait_recv()
    stat_out[...] = stat_mine[...] + stat_other[...]
    for half in range(2):
        stats(half).wait_send()
        store(half).wait()


def norm_kernel(
    width, stream_ref, stat_ref, mod_ref, hid_ref, mlp_ref,
    stream_in, stat, mod, hid, mlp, load_sems, sems,
):
    tile = 64
    count = stream_ref.shape[0] // tile
    load_mod = pltpu.make_async_copy(mod_ref, mod, load_sems.at[count])
    load_stat = pltpu.make_async_copy(stat_ref, stat, load_sems.at[count + 1])
    load_mod.start()
    load_stat.start()
    loads = []
    for i in range(count):
        at = pl.ds(i * tile, tile)
        loads.append(
            pltpu.make_async_copy(stream_ref.at[at], stream_in.at[at], load_sems.at[i])
        )
        loads[i].start()
    load_mod.wait()
    load_stat.wait()
    shift = mod[0:1, :]
    scale = 1.0 + mod[1:2, :]
    copies = []
    for i in range(count):
        at = pl.ds(i * tile, tile)
        loads[i].wait()
        stream = stream_in[at, :]
        mean = stat[at, 0:1] / width
        var = stat[at, 64:65] / width - mean * mean
        hid[at, :] = stream.astype(jnp.bfloat16)
        result = (stream - mean) * lax.rsqrt(var + 1e-06) * scale + shift
        mlp[at, :] = result.astype(jnp.bfloat16)
        for k, (source, target) in enumerate(((hid, hid_ref), (mlp, mlp_ref))):
            copy = pltpu.make_async_copy(source.at[at], target.at[at], sems.at[k, i])
            copy.start()
            copies.append(copy)
    for copy in copies:
        copy.wait()


def fused(n, mp_n, residual, queries, keys, values, video_ids, timestep, modulation, out_weight):
    rows, width = queries.shape
    high, columns = residual.shape
    tokens = rows * n
    groups = width // HEAD_DIM // n
    steps = modulation.shape[0]
    bf16, f32 = jnp.bfloat16, jnp.float32
    dma = pltpu.SemaphoreType.DMA
    hbm = pl.BlockSpec(memory_space=pltpu.HBM)
    smem = pl.BlockSpec(memory_space=pltpu.SMEM)
    vmem = pl.BlockSpec(memory_space=pltpu.VMEM)
    stream, stat, mods = pl.pallas_call(
        functools.partial(fused_kernel, n, mp_n),
        out_shape=(
            jax.ShapeDtypeStruct((high, columns), f32),
            jax.ShapeDtypeStruct((high, 128), f32),
            jax.ShapeDtypeStruct((2, columns), f32),
        ),
        in_specs=[hbm, hbm, hbm, hbm, smem, hbm, hbm, hbm],
        out_specs=(hbm, vmem, vmem),
        scratch_shapes=[
            pltpu.VMEM((high, columns), f32),
            pltpu.VMEM((groups, 3, n, rows, HEAD_DIM), bf16),
            pltpu.VMEM((groups, 3, tokens, HEAD_DIM), bf16),
            pltpu.VMEM((tokens, HEAD_DIM), bf16),
            pltpu.VMEM((tokens, HEAD_DIM), bf16),
            pltpu.VMEM((HEAD_DIM + 16, tokens), bf16),
            pltpu.VMEM((groups, tokens, HEAD_DIM), bf16),
            pltpu.VMEM((groups, high, n * HEAD_DIM), bf16),
            pltpu.VMEM((groups, n * HEAD_DIM, columns), bf16),
            pltpu.VMEM((high, columns), bf16),
            pltpu.VMEM((3, steps, columns), f32),
            pltpu.VMEM((1, rows), jnp.int32),
            pltpu.VMEM((8 * n, 128), f32),
            pltpu.VMEM((high, 128), f32),
            pltpu.VMEM((high, 128), f32),
            dma((groups, 2)), dma((groups, 2)), dma((groups,)), dma((groups,)),
            dma((groups,)), dma((groups, n)), dma((groups,)), dma((groups,)),
            dma, dma, dma((2,)), dma((2,)), dma((groups,)), dma((3,)),
            dma((2,)),
        ],
        compiler_params=pltpu.CompilerParams(
            collective_id=0, has_side_effects=True, vmem_limit_bytes=56 * 2**20
        ),
    )(
        queries, keys, values, video_ids.reshape(1, rows), timestep,
        modulation.transpose(1, 0, 2), residual, out_weight,
    )
    out = jax.ShapeDtypeStruct(residual.shape, bf16)
    return pl.pallas_call(
        functools.partial(norm_kernel, width),
        out_shape=(out, out),
        in_specs=[hbm, hbm, hbm],
        out_specs=(hbm, hbm),
        scratch_shapes=[
            pltpu.VMEM((high, columns), f32),
            pltpu.VMEM((high, 128), f32),
            pltpu.VMEM((2, columns), f32),
            pltpu.VMEM((high, columns), bf16),
            pltpu.VMEM((high, columns), bf16),
            dma((high // 64 + 2,)),
            dma((2, high // 64)),
        ],
        compiler_params=pltpu.CompilerParams(vmem_limit_bytes=56 * 2**20),
    )(stream, stat, mods)


def attend(carry, q_rows, q_ids, key_rows, value_rows, key_ids):
    top, total, summed = carry
    rows = q_rows.shape[0]
    count = key_rows.shape[0]
    heads = q_rows.shape[1] // HEAD_DIM
    factor = 1.0 / HEAD_DIM**0.5
    q_heads = q_rows.reshape(rows, heads, HEAD_DIM)
    k_heads = key_rows.reshape(count, heads, HEAD_DIM)
    v_heads = value_rows.reshape(count, heads, HEAD_DIM)
    same = (q_ids[:, None] == key_ids[None, :])[None]
    new_top, new_total, new_summed = ([], [], [])
    for first in range(0, heads, 3):
        score = (
            jnp.einsum(
                "thd,nhd->htn",
                q_heads[:, first : first + 3],
                k_heads[:, first : first + 3],
                preferred_element_type=jnp.float32,
            )
            * factor
        )
        score = jnp.where(same, score, -1e30)
        old_top = top[first : first + 3]
        peak = jnp.maximum(old_top, jnp.max(score, axis=2))
        weight = jnp.where(same, jnp.exp(score - peak[:, :, None]), 0.0)
        new_top.append(peak)
        new_total.append(jnp.sum(weight, axis=2))
        part_sum = jnp.einsum(
            "htn,nhd->htd",
            weight.astype(jnp.bfloat16),
            v_heads[:, first : first + 3],
            preferred_element_type=jnp.float32,
        )
        new_summed.append(part_sum)
    return (
        jnp.concatenate(new_top, 0),
        jnp.concatenate(new_total, 0),
        jnp.concatenate(new_summed, 0),
    )


def attend_maybe(carry, q_rows, q_ids, key_rows, value_rows, key_ids):
    return attend(carry, q_rows, q_ids, key_rows, value_rows, key_ids)


def start_state(q_rows):
    rows = q_rows.shape[0]
    heads = q_rows.shape[1] // HEAD_DIM
    return (
        jnp.full((heads, rows), -1e30, jnp.float32),
        jnp.zeros((heads, rows), jnp.float32),
        jnp.zeros((heads, rows, HEAD_DIM), jnp.float32),
    )


def finish(state, q_rows):
    top, total, summed = state
    rows = q_rows.shape[0]
    heads = q_rows.shape[1] // HEAD_DIM
    result = summed / total[:, :, None]
    return result.transpose(1, 0, 2).reshape(rows, heads * HEAD_DIM).astype(jnp.bfloat16)


def local(residual, queries, keys, values, video_ids, timestep, modulation, out_weight):
    steps_count = modulation.shape[0]
    picker = (jnp.arange(steps_count, dtype=jnp.int32) == timestep[0]).astype(jnp.float32)
    mod_rows = jnp.einsum("s,scd->cd", picker, modulation, precision=lax.Precision.HIGHEST)
    gate = mod_rows[0]
    shift = mod_rows[1]
    scale = mod_rows[2]
    width = queries.shape[1]
    state = attend_maybe(
        start_state(queries),
        queries,
        video_ids,
        lax.all_gather(keys, ("seq", "mp"), axis=0, tiled=True),
        lax.all_gather(values, ("seq", "mp"), axis=0, tiled=True),
        lax.all_gather(video_ids, ("seq", "mp"), axis=0, tiled=True),
    )
    attended = finish(state, queries)
    projected = jnp.dot(
        lax.all_gather(attended, "mp", axis=0, tiled=True),
        out_weight,
        preferred_element_type=jnp.float32,
    )
    stream = residual.astype(jnp.float32) + gate[None, :] * projected
    row_sum = jnp.sum(stream, axis=1, keepdims=True)
    row_sq = jnp.sum(stream * stream, axis=1, keepdims=True)
    row_sum, row_sq = lax.psum((row_sum, row_sq), "mp")
    mean = row_sum / width
    var = row_sq / width - mean * mean
    normed = (stream - mean) * lax.rsqrt(var + 1e-06) * (1.0 + scale[None, :]) + shift[None, :]
    return (stream.astype(jnp.bfloat16), normed.astype(jnp.bfloat16))


def choose(mesh):
    seq_n, mp_n = mesh.shape["seq"], mesh.shape["mp"]
    n = seq_n * mp_n

    def run(*arrays):
        queries = arrays[1]
        rows, width = queries.shape
        if mp_n == 2 and width // HEAD_DIM % n == 0 and rows % 64 == 0 and rows * n % 512 == 0:
            return fused(n, mp_n, *arrays)
        return local(*arrays)

    return run


def solution(mesh):
    return jax.shard_map(
        choose(mesh),
        mesh=mesh,
        in_specs=(
            P(("dp", "seq"), "mp"),
            P(("dp", "seq", "mp"), None),
            P(("dp", "seq", "mp"), None),
            P(("dp", "seq", "mp"), None),
            P(("dp", "seq", "mp")),
            P("dp"),
            P(None, None, "mp"),
            P(None, "mp"),
        ),
        out_specs=(P(("dp", "seq"), "mp"), P(("dp", "seq"), "mp")),
        check_vma=False,
    )
```

```python
import functools

import jax
import jax.numpy as jnp
from jax import lax
from jax.experimental import pallas as pl
from jax.experimental.pallas import tpu as pltpu
from jax.sharding import PartitionSpec as P

HEAD_DIM = 128
VIDEOS = 4
MARK = 2.0**50
MESH = pl.DeviceIdType.MESH


def rows_at(index, count):
    return pl.ds(pl.multiple_of(index * count, count), count)


def whole(ref, sem):
    return pltpu.make_async_copy(ref, ref, sem)


def fused_kernel(
    n, mp_n,
    q_ref, k_ref, v_ref, ids_ref, step_ref, mod_ref, res_ref, w_ref,
    stream_ref, stat_out, mod_out,
    acc, keys_values, queries, key_marks, query_marks, values_t, obuf, att, wbuf, res,
    mods, ids_mine, counts, stat_mine, stat_other,
    x_send, kv_recv, q_recv, y_send, y_recv, o_send, o_recv, fwd_send, fwd_recv,
    cnt_send, cnt_recv, stat_send, stat_recv, w_sem, in_sem, out_sem,
):
    seq_i = lax.axis_index("seq")
    mp_i = lax.axis_index("mp")
    me = seq_i * mp_n + mp_i
    row_n = n // 2
    my_y = lax.div(me, row_n)
    mine = lax.rem(me, row_n)
    rows = q_ref.shape[0]
    groups, half_tokens = queries.shape[0], queries.shape[1]
    tokens = 2 * half_tokens
    columns = w_ref.shape[1]
    sibling = {"mp": 1 - mp_i}
    opposite = {"seq": lax.rem(seq_i + row_n // mp_n, n // mp_n)}

    def device(p):
        return {"seq": lax.div(p, mp_n), "mp": lax.rem(p, mp_n)}

    def in_row(r):
        return device(my_y * row_n + r)

    def each_peer(body):
        def step(d, carry):
            body(lax.rem(me + d, n))
            return carry

        lax.fori_loop(1, n, step, 0)

    def row_peers(body):
        def step(d, carry):
            body(lax.rem(mine + d, row_n))
            return carry

        lax.fori_loop(1, row_n, step, 0)

    def head(r, g):
        return rows_at(r * groups + g, HEAD_DIM)

    def own_block(r):
        return rows_at(my_y * row_n + r, rows)

    def send_row(g):
        for t, ref in enumerate((k_ref, v_ref, q_ref)):
            if t < 2:
                there, sem = keys_values.at[g, t, own_block(mine)], kv_recv.at[g, mine]
            else:
                there, sem = queries.at[g, rows_at(mine, rows)], q_recv.at[g]

            def send(r, ref=ref, there=there, sem=sem):
                pltpu.make_async_remote_copy(
                    src_ref=ref.at[:, head(r, g)],
                    dst_ref=there,
                    send_sem=x_send.at[g],
                    recv_sem=sem,
                    device_id=in_row(r),
                    device_id_type=MESH,
                ).start()

            pltpu.make_async_copy(ref.at[:, head(mine, g)], there, sem).start()
            row_peers(send)

    def send_across(g, r):
        block = keys_values.at[g, :, own_block(r)]
        whole(block, kv_recv.at[g, r]).wait()
        pltpu.make_async_remote_copy(
            src_ref=block,
            dst_ref=block,
            send_sem=y_send.at[g],
            recv_sem=y_recv.at[g],
            device_id=opposite,
            device_id_type=MESH,
        ).start()

    def across_near(g):
        send_across(g, mine)
        send_across(g, mine + 1 - 2 * mp_i)

    def across_far(g):
        first = lax.rem(lax.div(mine, mp_n) + 1, row_n // mp_n) * mp_n
        for core in range(mp_n):
            send_across(g, first + core)

    barrier = pltpu.get_barrier_semaphore()
    each_peer(
        lambda p: pl.semaphore_signal(
            barrier, inc=1, device_id=device(p), device_id_type=MESH
        )
    )
    load_ids = pltpu.make_async_copy(ids_ref, ids_mine, in_sem.at[0])
    load_res = pltpu.make_async_copy(res_ref, res, in_sem.at[1])
    load_mods = pltpu.make_async_copy(mod_ref, mods, in_sem.at[2])
    load_ids.start()
    pl.semaphore_wait(barrier, n - 1)

    ahead = 3
    for g in range(ahead):
        send_row(g)

    load_ids.wait()
    ids = ids_mine[...]
    below = [
        jnp.sum((ids <= k).astype(jnp.float32), axis=1, keepdims=True)
        for k in range(VIDEOS - 1)
    ]
    line = lax.broadcasted_iota(jnp.int32, (8, 128), 0)
    counts[rows_at(me, 8), :] = jnp.where(
        line == 0, below[0], jnp.where(line == 1, below[1], below[2])
    )

    def send_count(p):
        pltpu.make_async_remote_copy(
            src_ref=counts.at[rows_at(me, 8)],
            dst_ref=counts.at[rows_at(me, 8)],
            send_sem=cnt_send,
            recv_sem=cnt_recv,
            device_id=device(p),
            device_id_type=MESH,
        ).start()

    each_peer(send_count)
    across_near(0)
    across_near(1)
    load_res.start()
    load_mods.start()

    def load_weight(i, carry):
        g, r = lax.div(i, row_n), lax.rem(i, row_n)
        pltpu.make_async_copy(
            w_ref.at[head(r, g)], wbuf.at[g, rows_at(r, HEAD_DIM)], w_sem.at[g]
        ).start()
        return carry

    lax.fori_loop(0, groups * row_n, load_weight, 0)
    acc[...] = jnp.zeros_like(acc)

    whole(counts.at[pl.ds(0, 8 * (n - 1))], cnt_recv).wait()
    sums = counts[pl.ds(0, 8), :]
    for r in range(1, n):
        sums = sums + counts[pl.ds(8 * r, 8), :]
    totals = [sums[k : k + 1, 0:1] for k in range(VIDEOS - 1)]
    tile = 2 * HEAD_DIM

    def mark(i, carry):
        at = rows_at(i, tile)
        place = (lax.broadcasted_iota(jnp.int32, (tile, 1), 0) + i * tile).astype(
            jnp.float32
        )
        own = sum((place >= c).astype(jnp.float32) for c in totals)
        video = lax.broadcasted_iota(jnp.int32, (tile, HEAD_DIM), 1).astype(jnp.float32)
        key_marks[at, :] = jnp.where(own == video, -MARK, 0.0).astype(jnp.bfloat16)
        other = jnp.where(own == video, 0.0, MARK)
        query_marks[at, :] = jnp.where(video < VIDEOS, other, 0.0).astype(jnp.bfloat16)
        return carry

    lax.fori_loop(0, tokens // tile, mark, 0)
    values_t[HEAD_DIM:, :] = jnp.ones((values_t.shape[0] - HEAD_DIM, tokens), jnp.bfloat16)
    across_far(0)

    def attention(g):
        values_t[:HEAD_DIM, :] = keys_values[g, 1].T
        for i in range(half_tokens // tile):
            at = pl.ds(i * tile, tile)
            marks = pl.ds(pl.multiple_of(my_y * half_tokens + i * tile, tile), tile)
            score = lax.dot_general(
                jnp.concatenate([keys_values[g, 0], key_marks[...]], axis=1),
                jnp.concatenate([queries[g, at, :], query_marks[marks, :]], axis=1),
                (((1,), (1,)), ((), ())),
                preferred_element_type=jnp.float32,
            )
            top = jnp.max(score, axis=0, keepdims=True)
            weight = jnp.exp((score - top) * (1.0 / HEAD_DIM**0.5)).astype(jnp.bfloat16)
            summed = jnp.dot(values_t[...], weight, preferred_element_type=jnp.float32)
            result = summed[:HEAD_DIM] / summed[HEAD_DIM : HEAD_DIM + 1]
            obuf[g, at, :] = result.T.astype(jnp.bfloat16)

    def send_back(g):
        def landing(r):
            return att.at[g, rows_at(lax.rem(r, mp_n), rows), rows_at(mine, HEAD_DIM)]

        def send(r):
            pltpu.make_async_remote_copy(
                src_ref=obuf.at[g, rows_at(r, rows)],
                dst_ref=landing(r),
                send_sem=o_send.at[g],
                recv_sem=o_recv.at[g, mine],
                device_id=in_row(r),
                device_id_type=MESH,
            ).start()

        row_peers(send)
        pltpu.make_async_copy(
            obuf.at[g, rows_at(mine, rows)], landing(mine), o_recv.at[g, mine]
        ).start()

    def pass_on(g):
        def step(d, carry):
            r = lax.rem(mine + d, row_n)
            block = att.at[g, rows_at(mp_i, rows), rows_at(r, HEAD_DIM)]
            whole(block, o_recv.at[g, r]).wait()
            pltpu.make_async_remote_copy(
                src_ref=block,
                dst_ref=block,
                send_sem=fwd_send.at[g],
                recv_sem=fwd_recv.at[g],
                device_id=sibling,
                device_id_type=MESH,
            ).start()
            return carry

        lax.fori_loop(0, row_n, step, 0)

    def project(g, half):
        rows_of = rows_at(half, rows)

        def step(i, carry):
            at = rows_at(i, tile)
            acc[rows_of, at] += jnp.dot(
                att[g, rows_of, :], wbuf[g, :, at], preferred_element_type=jnp.float32
            )
            return carry

        lax.fori_loop(0, columns // tile, step, 0)

    def wait_forward(g):
        whole(att.at[g, rows_at(1 - mp_i, rows)], fwd_recv.at[g]).wait()

    def project_both(g):
        whole(wbuf.at[g], w_sem.at[g]).wait()
        wait_forward(g)
        project(g, mp_i)
        project(g, 1 - mp_i)

    def group(g, carry):
        @pl.when(g + ahead < groups)
        def _():
            send_row(g + ahead)

        @pl.when(g + 2 < groups)
        def _():
            across_near(g + 2)

        @pl.when(g + 1 < groups)
        def _():
            across_far(g + 1)

        other = keys_values.at[g, :, rows_at(1 - my_y, half_tokens)]
        whole(other, y_recv.at[g]).wait()
        whole(queries.at[g], q_recv.at[g]).wait()
        attention(g)
        send_back(g)

        @pl.when(g >= 1)
        def _():
            pass_on(g - 1)

        @pl.when(g >= 2)
        def _():
            project_both(g - 2)

        return carry

    lax.fori_loop(0, groups, group, 0)
    last = groups - 1
    project_both(last - 1)
    pass_on(last)

    load_res.wait()
    load_mods.wait()
    chosen = step_ref[0]
    gate = mods[0, pl.ds(chosen, 1), :]
    mod_out[0:1, :] = mods[1, pl.ds(chosen, 1), :]
    mod_out[1:2, :] = mods[2, pl.ds(chosen, 1), :]
    strip = rows // 3 if rows % 48 == 0 else 16
    side = lax.broadcasted_iota(jnp.int32, (strip, 128), 1) < 64

    def stats(half):
        part = rows_at(half, rows)
        return pltpu.make_async_remote_copy(
            src_ref=stat_mine.at[part],
            dst_ref=stat_other.at[part],
            send_sem=stat_send.at[half],
            recv_sem=stat_recv.at[half],
            device_id=sibling,
            device_id_type=MESH,
        )

    def store(half):
        part = rows_at(half, rows)
        return pltpu.make_async_copy(acc.at[part], stream_ref.at[part], out_sem.at[half])

    def finish(half):
        project(last, half)

        def gated(i, carry):
            at = rows_at(half * (rows // strip) + i, strip)
            stream = res[at, :].astype(jnp.float32) + gate * acc[at, :]
            acc[at, :] = stream
            row_sum = jnp.sum(stream, axis=1, keepdims=True)
            row_sq = jnp.sum(stream * stream, axis=1, keepdims=True)
            stat_mine[at, :] = jnp.where(side, row_sum, row_sq)
            return carry

        lax.fori_loop(0, rows // strip, gated, 0)
        stats(half).start()
        store(half).start()

    whole(wbuf.at[last], w_sem.at[last]).wait()
    finish(mp_i)
    wait_forward(last)
    finish(1 - mp_i)

    whole(counts.at[pl.ds(0, 8 * (n - 1))], cnt_send).wait()

    def drain(g, carry):
        whole(obuf.at[g, pl.ds(0, rows * (row_n - 1))], o_send.at[g]).wait()
        whole(keys_values.at[g, :, pl.ds(0, half_tokens)], y_send.at[g]).wait()
        whole(queries.at[pl.ds(0, 3), pl.ds(0, rows * (row_n - 1))], x_send.at[g]).wait()
        whole(att.at[g, rows_at(mp_i, rows)], fwd_send.at[g]).wait()
        return carry

    lax.fori_loop(0, groups, drain, 0)
    for half in range(2):
        stats(half).wait_recv()
    stat_out[...] = stat_mine[...] + stat_other[...]
    for half in range(2):
        stats(half).wait_send()
        store(half).wait()


def norm_kernel(
    width, stream_ref, stat_ref, mod_ref, hid_ref, mlp_ref,
    stream_in, stat, mod, hid, mlp, load_sems, sems,
):
    tile = 64
    count = stream_ref.shape[0] // tile
    load_mod = pltpu.make_async_copy(mod_ref, mod, load_sems.at[count])
    load_stat = pltpu.make_async_copy(stat_ref, stat, load_sems.at[count + 1])
    load_mod.start()
    load_stat.start()
    loads = []
    for i in range(count):
        at = pl.ds(i * tile, tile)
        loads.append(
            pltpu.make_async_copy(stream_ref.at[at], stream_in.at[at], load_sems.at[i])
        )
        loads[i].start()
    load_mod.wait()
    load_stat.wait()
    shift = mod[0:1, :]
    scale = 1.0 + mod[1:2, :]
    copies = []
    for i in range(count):
        at = pl.ds(i * tile, tile)
        loads[i].wait()
        stream = stream_in[at, :]
        mean = stat[at, 0:1] / width
        var = stat[at, 64:65] / width - mean * mean
        hid[at, :] = stream.astype(jnp.bfloat16)
        result = (stream - mean) * lax.rsqrt(var + 1e-06) * scale + shift
        mlp[at, :] = result.astype(jnp.bfloat16)
        for k, (source, target) in enumerate(((hid, hid_ref), (mlp, mlp_ref))):
            copy = pltpu.make_async_copy(source.at[at], target.at[at], sems.at[k, i])
            copy.start()
            copies.append(copy)
    for copy in copies:
        copy.wait()


def fused(n, mp_n, residual, queries, keys, values, video_ids, timestep, modulation, out_weight):
    rows, width = queries.shape
    high, columns = residual.shape
    tokens = rows * n
    row_n = n // 2
    groups = width // HEAD_DIM // row_n
    steps = modulation.shape[0]
    bf16, f32 = jnp.bfloat16, jnp.float32
    dma = pltpu.SemaphoreType.DMA
    hbm = pl.BlockSpec(memory_space=pltpu.HBM)
    smem = pl.BlockSpec(memory_space=pltpu.SMEM)
    vmem = pl.BlockSpec(memory_space=pltpu.VMEM)
    stream, stat, mods = pl.pallas_call(
        functools.partial(fused_kernel, n, mp_n),
        out_shape=(
            jax.ShapeDtypeStruct((high, columns), f32),
            jax.ShapeDtypeStruct((high, 128), f32),
            jax.ShapeDtypeStruct((2, columns), f32),
        ),
        in_specs=[hbm, hbm, hbm, hbm, smem, hbm, hbm, hbm],
        out_specs=(hbm, vmem, vmem),
        scratch_shapes=[
            pltpu.VMEM((high, columns), f32),
            pltpu.VMEM((groups, 2, tokens, HEAD_DIM), bf16),
            pltpu.VMEM((groups, tokens // 2, HEAD_DIM), bf16),
            pltpu.VMEM((tokens, HEAD_DIM), bf16),
            pltpu.VMEM((tokens, HEAD_DIM), bf16),
            pltpu.VMEM((HEAD_DIM + 16, tokens), bf16),
            pltpu.VMEM((groups, tokens // 2, HEAD_DIM), bf16),
            pltpu.VMEM((groups, high, row_n * HEAD_DIM), bf16),
            pltpu.VMEM((groups, row_n * HEAD_DIM, columns), bf16),
            pltpu.VMEM((high, columns), bf16),
            pltpu.VMEM((3, steps, columns), f32),
            pltpu.VMEM((1, rows), jnp.int32),
            pltpu.VMEM((8 * n, 128), f32),
            pltpu.VMEM((high, 128), f32),
            pltpu.VMEM((high, 128), f32),
            dma((groups,)), dma((groups, row_n)), dma((groups,)), dma((groups,)),
            dma((groups,)), dma((groups,)), dma((groups, row_n)), dma((groups,)),
            dma((groups,)), dma, dma, dma((2,)), dma((2,)), dma((groups,)), dma((3,)),
            dma((2,)),
        ],
        compiler_params=pltpu.CompilerParams(
            collective_id=0, has_side_effects=True, vmem_limit_bytes=56 * 2**20
        ),
    )(
        queries, keys, values, video_ids.reshape(1, rows), timestep,
        modulation.transpose(1, 0, 2), residual, out_weight,
    )
    out = jax.ShapeDtypeStruct(residual.shape, bf16)
    return pl.pallas_call(
        functools.partial(norm_kernel, width),
        out_shape=(out, out),
        in_specs=[hbm, hbm, hbm],
        out_specs=(hbm, hbm),
        scratch_shapes=[
            pltpu.VMEM((high, columns), f32),
            pltpu.VMEM((high, 128), f32),
            pltpu.VMEM((2, columns), f32),
            pltpu.VMEM((high, columns), bf16),
            pltpu.VMEM((high, columns), bf16),
            dma((high // 64 + 2,)),
            dma((2, high // 64)),
        ],
        compiler_params=pltpu.CompilerParams(vmem_limit_bytes=56 * 2**20),
    )(stream, stat, mods)


def attend(carry, q_rows, q_ids, key_rows, value_rows, key_ids):
    top, total, summed = carry
    rows = q_rows.shape[0]
    count = key_rows.shape[0]
    heads = q_rows.shape[1] // HEAD_DIM
    factor = 1.0 / HEAD_DIM**0.5
    q_heads = q_rows.reshape(rows, heads, HEAD_DIM)
    k_heads = key_rows.reshape(count, heads, HEAD_DIM)
    v_heads = value_rows.reshape(count, heads, HEAD_DIM)
    same = (q_ids[:, None] == key_ids[None, :])[None]
    new_top, new_total, new_summed = ([], [], [])
    for first in range(0, heads, 3):
        score = (
            jnp.einsum(
                "thd,nhd->htn",
                q_heads[:, first : first + 3],
                k_heads[:, first : first + 3],
                preferred_element_type=jnp.float32,
            )
            * factor
        )
        score = jnp.where(same, score, -1e30)
        old_top = top[first : first + 3]
        peak = jnp.maximum(old_top, jnp.max(score, axis=2))
        weight = jnp.where(same, jnp.exp(score - peak[:, :, None]), 0.0)
        new_top.append(peak)
        new_total.append(jnp.sum(weight, axis=2))
        part_sum = jnp.einsum(
            "htn,nhd->htd",
            weight.astype(jnp.bfloat16),
            v_heads[:, first : first + 3],
            preferred_element_type=jnp.float32,
        )
        new_summed.append(part_sum)
    return (
        jnp.concatenate(new_top, 0),
        jnp.concatenate(new_total, 0),
        jnp.concatenate(new_summed, 0),
    )


def attend_maybe(carry, q_rows, q_ids, key_rows, value_rows, key_ids):
    return attend(carry, q_rows, q_ids, key_rows, value_rows, key_ids)


def start_state(q_rows):
    rows = q_rows.shape[0]
    heads = q_rows.shape[1] // HEAD_DIM
    return (
        jnp.full((heads, rows), -1e30, jnp.float32),
        jnp.zeros((heads, rows), jnp.float32),
        jnp.zeros((heads, rows, HEAD_DIM), jnp.float32),
    )


def finish(state, q_rows):
    top, total, summed = state
    rows = q_rows.shape[0]
    heads = q_rows.shape[1] // HEAD_DIM
    result = summed / total[:, :, None]
    return result.transpose(1, 0, 2).reshape(rows, heads * HEAD_DIM).astype(jnp.bfloat16)


def local(residual, queries, keys, values, video_ids, timestep, modulation, out_weight):
    steps_count = modulation.shape[0]
    picker = (jnp.arange(steps_count, dtype=jnp.int32) == timestep[0]).astype(jnp.float32)
    mod_rows = jnp.einsum("s,scd->cd", picker, modulation, precision=lax.Precision.HIGHEST)
    gate = mod_rows[0]
    shift = mod_rows[1]
    scale = mod_rows[2]
    width = queries.shape[1]
    state = attend_maybe(
        start_state(queries),
        queries,
        video_ids,
        lax.all_gather(keys, ("seq", "mp"), axis=0, tiled=True),
        lax.all_gather(values, ("seq", "mp"), axis=0, tiled=True),
        lax.all_gather(video_ids, ("seq", "mp"), axis=0, tiled=True),
    )
    attended = finish(state, queries)
    projected = jnp.dot(
        lax.all_gather(attended, "mp", axis=0, tiled=True),
        out_weight,
        preferred_element_type=jnp.float32,
    )
    stream = residual.astype(jnp.float32) + gate[None, :] * projected
    row_sum = jnp.sum(stream, axis=1, keepdims=True)
    row_sq = jnp.sum(stream * stream, axis=1, keepdims=True)
    row_sum, row_sq = lax.psum((row_sum, row_sq), "mp")
    mean = row_sum / width
    var = row_sq / width - mean * mean
    normed = (stream - mean) * lax.rsqrt(var + 1e-06) * (1.0 + scale[None, :]) + shift[None, :]
    return (stream.astype(jnp.bfloat16), normed.astype(jnp.bfloat16))


def choose(mesh):
    seq_n, mp_n = mesh.shape["seq"], mesh.shape["mp"]
    n = seq_n * mp_n

    def run(*arrays):
        queries = arrays[1]
        rows, width = queries.shape
        even = rows % 64 == 0 and rows * n % 512 == 0 and width // HEAD_DIM % (n // 2) == 0
        if mp_n == 2 and seq_n == 4 and even and width // HEAD_DIM // (n // 2) >= 3:
            return fused(n, mp_n, *arrays)
        return local(*arrays)

    return run


def solution(mesh):
    return jax.shard_map(
        choose(mesh),
        mesh=mesh,
        in_specs=(
            P(("dp", "seq"), "mp"),
            P(("dp", "seq", "mp"), None),
            P(("dp", "seq", "mp"), None),
            P(("dp", "seq", "mp"), None),
            P(("dp", "seq", "mp")),
            P("dp"),
            P(None, None, "mp"),
            P(None, "mp"),
        ),
        out_specs=(P(("dp", "seq"), "mp"), P(("dp", "seq"), "mp")),
        check_vma=False,
    )
```

```python
import functools

import jax
import jax.numpy as jnp
from jax import lax
from jax.experimental import pallas as pl
from jax.experimental.pallas import tpu as pltpu
from jax.sharding import PartitionSpec as P

HEAD_DIM = 128
VIDEOS = 4
MARK = 2.0**50
MESH = pl.DeviceIdType.MESH


def rows_at(index, count):
    return pl.ds(pl.multiple_of(index * count, count), count)


def whole(ref, sem):
    return pltpu.make_async_copy(ref, ref, sem)


def fused_kernel(
    n, mp_n,
    q_ref, k_ref, v_ref, ids_ref, step_ref, mod_ref, res_ref, w_ref,
    stream_ref, stat_out, mod_out,
    acc, qkv, key_marks, query_marks, values_t, obuf, att, wbuf, res, mods, ids_mine, counts,
    stat_mine, stat_other,
    qkv_send, qkv_recv, o_send, o_recv, fwd_send, fwd_recv,
    cnt_send, cnt_recv, stat_send, stat_recv, w_sem, in_sem, out_sem,
):
    seq_i = lax.axis_index("seq")
    mp_i = lax.axis_index("mp")
    me = seq_i * mp_n + mp_i
    rows = q_ref.shape[0]
    groups = qkv.shape[0]
    tokens = qkv.shape[2]
    columns = w_ref.shape[1]
    sibling = {"mp": 1 - mp_i}

    def device(p):
        return {"seq": lax.div(p, mp_n), "mp": lax.rem(p, mp_n)}

    def each_peer(body):
        def step(d, carry):
            body(lax.rem(me + d, n))
            return carry

        lax.fori_loop(1, n, step, 0)

    def every(body):
        def step(p, carry):
            body(p)
            return carry

        lax.fori_loop(0, n, step, 0)

    def send_group(g):
        for t, ref in enumerate((k_ref, q_ref, v_ref)):

            def send(p, ref=ref, t=t):
                pltpu.make_async_remote_copy(
                    src_ref=ref.at[:, rows_at(p * groups + g, HEAD_DIM)],
                    dst_ref=qkv.at[g, t, rows_at(me, rows)],
                    send_sem=qkv_send.at[g],
                    recv_sem=qkv_recv.at[g],
                    device_id=device(p),
                    device_id_type=MESH,
                ).start()

            each_peer(send)
            pltpu.make_async_copy(
                ref.at[:, rows_at(me * groups + g, HEAD_DIM)],
                qkv.at[g, t, rows_at(me, rows)],
                qkv_recv.at[g],
            ).start()

    barrier = pltpu.get_barrier_semaphore()
    each_peer(
        lambda p: pl.semaphore_signal(
            barrier, inc=1, device_id=device(p), device_id_type=MESH
        )
    )
    load_ids = pltpu.make_async_copy(ids_ref, ids_mine, in_sem.at[0])
    load_res = pltpu.make_async_copy(res_ref, res, in_sem.at[1])
    load_mods = pltpu.make_async_copy(mod_ref, mods, in_sem.at[2])
    load_ids.start()
    pl.semaphore_wait(barrier, n - 1)

    ahead = 2
    for g in range(min(ahead, groups)):
        send_group(g)

    load_ids.wait()
    ids = ids_mine[...]
    below = [
        jnp.sum((ids <= k).astype(jnp.float32), axis=1, keepdims=True)
        for k in range(VIDEOS - 1)
    ]
    line = lax.broadcasted_iota(jnp.int32, (8, 128), 0)
    mine = jnp.where(line == 0, below[0], jnp.where(line == 1, below[1], below[2]))
    counts[rows_at(me, 8), :] = mine

    def send_count(p):
        pltpu.make_async_remote_copy(
            src_ref=counts.at[rows_at(me, 8)],
            dst_ref=counts.at[rows_at(me, 8)],
            send_sem=cnt_send,
            recv_sem=cnt_recv,
            device_id=device(p),
            device_id_type=MESH,
        ).start()

    each_peer(send_count)
    load_res.start()
    load_mods.start()
    for g in range(groups):

        def load_weight(p, g=g):
            pltpu.make_async_copy(
                w_ref.at[rows_at(p * groups + g, HEAD_DIM)],
                wbuf.at[g, rows_at(p, HEAD_DIM)],
                w_sem.at[g],
            ).start()

        every(load_weight)

    whole(counts.at[pl.ds(0, 8 * (n - 1))], cnt_recv).wait()
    sums = counts[pl.ds(0, 8), :]
    for r in range(1, n):
        sums = sums + counts[pl.ds(8 * r, 8), :]
    totals = [sums[k : k + 1, 0:1] for k in range(VIDEOS - 1)]
    tile = 2 * HEAD_DIM

    def mark(i, carry):
        at = rows_at(i, tile)
        place = (lax.broadcasted_iota(jnp.int32, (tile, 1), 0) + i * tile).astype(
            jnp.float32
        )
        own = sum((place >= c).astype(jnp.float32) for c in totals)
        video = lax.broadcasted_iota(jnp.int32, (tile, HEAD_DIM), 1).astype(jnp.float32)
        key_marks[at, :] = jnp.where(own == video, -MARK, 0.0).astype(jnp.bfloat16)
        other = jnp.where(own == video, 0.0, MARK)
        query_marks[at, :] = jnp.where(video < VIDEOS, other, 0.0).astype(jnp.bfloat16)
        return carry

    lax.fori_loop(0, tokens // tile, mark, 0)
    values_t[HEAD_DIM:, :] = jnp.ones((values_t.shape[0] - HEAD_DIM, tokens), jnp.bfloat16)
    chunk = tokens // 2
    peers = n // 2

    def attend_tile(g, start):
        at = pl.ds(pl.multiple_of(start, tile), tile)
        score = lax.dot_general(
            jnp.concatenate([qkv[g, 0], key_marks[...]], axis=1),
            jnp.concatenate([qkv[g, 1, at, :], query_marks[at, :]], axis=1),
            (((1,), (1,)), ((), ())),
            preferred_element_type=jnp.float32,
        )
        top = jnp.max(score, axis=0, keepdims=True)
        weight = jnp.exp((score - top) * (1.0 / HEAD_DIM**0.5)).astype(jnp.bfloat16)
        summed = jnp.dot(values_t[...], weight, preferred_element_type=jnp.float32)
        result = summed[:HEAD_DIM] / summed[HEAD_DIM : HEAD_DIM + 1]
        obuf[g, at, :] = result.T.astype(jnp.bfloat16)

    def attend_and_send(g):
        values_t[:HEAD_DIM, :] = qkv[g, 2].T

        def half(j, carry):
            part = lax.rem(lax.div(me, peers) + 1 + j, 2)
            for i in range(chunk // tile):
                attend_tile(g, part * chunk + i * tile)

            def send(d, carry):
                p = part * peers + lax.rem(me + d, peers)
                block = obuf.at[g, rows_at(p, rows)]
                there = att.at[
                    g, rows_at(lax.rem(p, mp_n), rows), rows_at(me, HEAD_DIM)
                ]

                @pl.when(p != me)
                def _():
                    pltpu.make_async_remote_copy(
                        src_ref=block,
                        dst_ref=there,
                        send_sem=o_send.at[g],
                        recv_sem=o_recv.at[g, me],
                        device_id=device(p),
                        device_id_type=MESH,
                    ).start()

                @pl.when(p == me)
                def _():
                    pltpu.make_async_copy(block, there, o_recv.at[g, me]).start()

                return carry

            return lax.fori_loop(0, peers, send, carry)

        lax.fori_loop(0, 2, half, 0)

    def pass_on(g):
        def step(d, carry):
            p = lax.rem(me + n - d, n)
            block = att.at[g, rows_at(mp_i, rows), rows_at(p, HEAD_DIM)]
            whole(block, o_recv.at[g, p]).wait()
            pltpu.make_async_remote_copy(
                src_ref=block,
                dst_ref=block,
                send_sem=fwd_send.at[g],
                recv_sem=fwd_recv.at[g],
                device_id=sibling,
                device_id_type=MESH,
            ).start()
            return carry

        lax.fori_loop(1, n + 1, step, 0)

    def project(g, half):
        rows_of = rows_at(half, rows)
        tile = 2 * HEAD_DIM

        def step(i, carry):
            at = rows_at(i, tile)
            part = jnp.dot(
                att[g, rows_of, :], wbuf[g, :, at], preferred_element_type=jnp.float32
            )
            acc[rows_of, at] = part if g == 0 else acc[rows_of, at] + part
            return carry

        lax.fori_loop(0, columns // tile, step, 0)

    def wait_forward(g):
        whole(att.at[g, rows_at(1 - mp_i, rows)], fwd_recv.at[g]).wait()

    def project_both(g):
        whole(wbuf.at[g], w_sem.at[g]).wait()
        wait_forward(g)
        project(g, mp_i)
        project(g, 1 - mp_i)

    for g in range(groups):
        whole(qkv.at[g], qkv_recv.at[g]).wait()
        if g + ahead < groups:
            send_group(g + ahead)
        attend_and_send(g)
        if g >= 1:
            pass_on(g - 1)
        if g >= 2:
            project_both(g - 2)
    if groups >= 2:
        project_both(groups - 2)
    last = groups - 1
    pass_on(last)

    load_res.wait()
    load_mods.wait()
    chosen = step_ref[0]
    gate = mods[0, pl.ds(chosen, 1), :]
    mod_out[0:1, :] = mods[1, pl.ds(chosen, 1), :]
    mod_out[1:2, :] = mods[2, pl.ds(chosen, 1), :]
    tile = rows // 3 if rows % 48 == 0 else 16
    side = lax.broadcasted_iota(jnp.int32, (tile, 128), 1) < 64

    def stats(half):
        part = rows_at(half, rows)
        return pltpu.make_async_remote_copy(
            src_ref=stat_mine.at[part],
            dst_ref=stat_other.at[part],
            send_sem=stat_send.at[half],
            recv_sem=stat_recv.at[half],
            device_id=sibling,
            device_id_type=MESH,
        )

    def store(half):
        part = rows_at(half, rows)
        return pltpu.make_async_copy(acc.at[part], stream_ref.at[part], out_sem.at[half])

    def finish(half):
        project(last, half)

        def gated(i, carry):
            at = rows_at(half * (rows // tile) + i, tile)
            stream = res[at, :].astype(jnp.float32) + gate * acc[at, :]
            acc[at, :] = stream
            row_sum = jnp.sum(stream, axis=1, keepdims=True)
            row_sq = jnp.sum(stream * stream, axis=1, keepdims=True)
            stat_mine[at, :] = jnp.where(side, row_sum, row_sq)
            return carry

        lax.fori_loop(0, rows // tile, gated, 0)
        stats(half).start()
        store(half).start()

    whole(wbuf.at[last], w_sem.at[last]).wait()
    finish(mp_i)
    wait_forward(last)
    finish(1 - mp_i)

    whole(counts.at[pl.ds(0, 8 * (n - 1))], cnt_send).wait()
    for g in range(groups):
        whole(qkv.at[g, :, pl.ds(0, rows * (n - 1))], qkv_send.at[g]).wait()
        whole(obuf.at[g, pl.ds(0, rows * (n - 1))], o_send.at[g]).wait()
        whole(att.at[g, rows_at(mp_i, rows)], fwd_send.at[g]).wait()
    for half in range(2):
        stats(half).wait_recv()
    stat_out[...] = stat_mine[...] + stat_other[...]
    for half in range(2):
        stats(half).wait_send()
        store(half).wait()


def norm_kernel(
    width, stream_ref, stat_ref, mod_ref, hid_ref, mlp_ref,
    stream_in, stat, mod, hid, mlp, load_sems, sems,
):
    tile = 64
    count = stream_ref.shape[0] // tile
    load_mod = pltpu.make_async_copy(mod_ref, mod, load_sems.at[count])
    load_stat = pltpu.make_async_copy(stat_ref, stat, load_sems.at[count + 1])
    load_mod.start()
    load_stat.start()
    loads = []
    for i in range(count):
        at = pl.ds(i * tile, tile)
        loads.append(
            pltpu.make_async_copy(stream_ref.at[at], stream_in.at[at], load_sems.at[i])
        )
        loads[i].start()
    load_mod.wait()
    load_stat.wait()
    shift = mod[0:1, :]
    scale = 1.0 + mod[1:2, :]
    copies = []
    for i in range(count):
        at = pl.ds(i * tile, tile)
        loads[i].wait()
        stream = stream_in[at, :]
        mean = stat[at, 0:1] / width
        var = stat[at, 64:65] / width - mean * mean
        hid[at, :] = stream.astype(jnp.bfloat16)
        result = (stream - mean) * lax.rsqrt(var + 1e-06) * scale + shift
        mlp[at, :] = result.astype(jnp.bfloat16)
        for k, (source, target) in enumerate(((hid, hid_ref), (mlp, mlp_ref))):
            copy = pltpu.make_async_copy(source.at[at], target.at[at], sems.at[k, i])
            copy.start()
            copies.append(copy)
    for copy in copies:
        copy.wait()


def fused(n, mp_n, residual, queries, keys, values, video_ids, timestep, modulation, out_weight):
    rows, width = queries.shape
    high, columns = residual.shape
    tokens = rows * n
    groups = width // HEAD_DIM // n
    steps = modulation.shape[0]
    bf16, f32 = jnp.bfloat16, jnp.float32
    dma = pltpu.SemaphoreType.DMA
    hbm = pl.BlockSpec(memory_space=pltpu.HBM)
    smem = pl.BlockSpec(memory_space=pltpu.SMEM)
    vmem = pl.BlockSpec(memory_space=pltpu.VMEM)
    stream, stat, mods = pl.pallas_call(
        functools.partial(fused_kernel, n, mp_n),
        out_shape=(
            jax.ShapeDtypeStruct((high, columns), f32),
            jax.ShapeDtypeStruct((high, 128), f32),
            jax.ShapeDtypeStruct((2, columns), f32),
        ),
        in_specs=[hbm, hbm, hbm, hbm, smem, hbm, hbm, hbm],
        out_specs=(hbm, vmem, vmem),
        scratch_shapes=[
            pltpu.VMEM((high, columns), f32),
            pltpu.VMEM((groups, 3, tokens, HEAD_DIM), bf16),
            pltpu.VMEM((tokens, HEAD_DIM), bf16),
            pltpu.VMEM((tokens, HEAD_DIM), bf16),
            pltpu.VMEM((HEAD_DIM + 16, tokens), bf16),
            pltpu.VMEM((groups, tokens, HEAD_DIM), bf16),
            pltpu.VMEM((groups, high, n * HEAD_DIM), bf16),
            pltpu.VMEM((groups, n * HEAD_DIM, columns), bf16),
            pltpu.VMEM((high, columns), bf16),
            pltpu.VMEM((3, steps, columns), f32),
            pltpu.VMEM((1, rows), jnp.int32),
            pltpu.VMEM((8 * n, 128), f32),
            pltpu.VMEM((high, 128), f32),
            pltpu.VMEM((high, 128), f32),
            dma((groups,)), dma((groups,)),
            dma((groups,)), dma((groups, n)), dma((groups,)), dma((groups,)),
            dma, dma, dma((2,)), dma((2,)), dma((groups,)), dma((3,)),
            dma((2,)),
        ],
        compiler_params=pltpu.CompilerParams(
            collective_id=0, has_side_effects=True, vmem_limit_bytes=56 * 2**20
        ),
    )(
        queries, keys, values, video_ids.reshape(1, rows), timestep,
        modulation.transpose(1, 0, 2), residual, out_weight,
    )
    out = jax.ShapeDtypeStruct(residual.shape, bf16)
    return pl.pallas_call(
        functools.partial(norm_kernel, width),
        out_shape=(out, out),
        in_specs=[hbm, hbm, hbm],
        out_specs=(hbm, hbm),
        scratch_shapes=[
            pltpu.VMEM((high, columns), f32),
            pltpu.VMEM((high, 128), f32),
            pltpu.VMEM((2, columns), f32),
            pltpu.VMEM((high, columns), bf16),
            pltpu.VMEM((high, columns), bf16),
            dma((high // 64 + 2,)),
            dma((2, high // 64)),
        ],
        compiler_params=pltpu.CompilerParams(vmem_limit_bytes=56 * 2**20),
    )(stream, stat, mods)


def attend(carry, q_rows, q_ids, key_rows, value_rows, key_ids):
    top, total, summed = carry
    rows = q_rows.shape[0]
    count = key_rows.shape[0]
    heads = q_rows.shape[1] // HEAD_DIM
    factor = 1.0 / HEAD_DIM**0.5
    q_heads = q_rows.reshape(rows, heads, HEAD_DIM)
    k_heads = key_rows.reshape(count, heads, HEAD_DIM)
    v_heads = value_rows.reshape(count, heads, HEAD_DIM)
    same = (q_ids[:, None] == key_ids[None, :])[None]
    new_top, new_total, new_summed = ([], [], [])
    for first in range(0, heads, 3):
        score = (
            jnp.einsum(
                "thd,nhd->htn",
                q_heads[:, first : first + 3],
                k_heads[:, first : first + 3],
                preferred_element_type=jnp.float32,
            )
            * factor
        )
        score = jnp.where(same, score, -1e30)
        old_top = top[first : first + 3]
        peak = jnp.maximum(old_top, jnp.max(score, axis=2))
        weight = jnp.where(same, jnp.exp(score - peak[:, :, None]), 0.0)
        new_top.append(peak)
        new_total.append(jnp.sum(weight, axis=2))
        part_sum = jnp.einsum(
            "htn,nhd->htd",
            weight.astype(jnp.bfloat16),
            v_heads[:, first : first + 3],
            preferred_element_type=jnp.float32,
        )
        new_summed.append(part_sum)
    return (
        jnp.concatenate(new_top, 0),
        jnp.concatenate(new_total, 0),
        jnp.concatenate(new_summed, 0),
    )


def attend_maybe(carry, q_rows, q_ids, key_rows, value_rows, key_ids):
    return attend(carry, q_rows, q_ids, key_rows, value_rows, key_ids)


def start_state(q_rows):
    rows = q_rows.shape[0]
    heads = q_rows.shape[1] // HEAD_DIM
    return (
        jnp.full((heads, rows), -1e30, jnp.float32),
        jnp.zeros((heads, rows), jnp.float32),
        jnp.zeros((heads, rows, HEAD_DIM), jnp.float32),
    )


def finish(state, q_rows):
    top, total, summed = state
    rows = q_rows.shape[0]
    heads = q_rows.shape[1] // HEAD_DIM
    result = summed / total[:, :, None]
    return result.transpose(1, 0, 2).reshape(rows, heads * HEAD_DIM).astype(jnp.bfloat16)


def local(residual, queries, keys, values, video_ids, timestep, modulation, out_weight):
    steps_count = modulation.shape[0]
    picker = (jnp.arange(steps_count, dtype=jnp.int32) == timestep[0]).astype(jnp.float32)
    mod_rows = jnp.einsum("s,scd->cd", picker, modulation, precision=lax.Precision.HIGHEST)
    gate = mod_rows[0]
    shift = mod_rows[1]
    scale = mod_rows[2]
    width = queries.shape[1]
    state = attend_maybe(
        start_state(queries),
        queries,
        video_ids,
        lax.all_gather(keys, ("seq", "mp"), axis=0, tiled=True),
        lax.all_gather(values, ("seq", "mp"), axis=0, tiled=True),
        lax.all_gather(video_ids, ("seq", "mp"), axis=0, tiled=True),
    )
    attended = finish(state, queries)
    projected = jnp.dot(
        lax.all_gather(attended, "mp", axis=0, tiled=True),
        out_weight,
        preferred_element_type=jnp.float32,
    )
    stream = residual.astype(jnp.float32) + gate[None, :] * projected
    row_sum = jnp.sum(stream, axis=1, keepdims=True)
    row_sq = jnp.sum(stream * stream, axis=1, keepdims=True)
    row_sum, row_sq = lax.psum((row_sum, row_sq), "mp")
    mean = row_sum / width
    var = row_sq / width - mean * mean
    normed = (stream - mean) * lax.rsqrt(var + 1e-06) * (1.0 + scale[None, :]) + shift[None, :]
    return (stream.astype(jnp.bfloat16), normed.astype(jnp.bfloat16))


def choose(mesh):
    seq_n, mp_n = mesh.shape["seq"], mesh.shape["mp"]
    n = seq_n * mp_n

    def run(*arrays):
        queries = arrays[1]
        rows, width = queries.shape
        if mp_n == 2 and width // HEAD_DIM % n == 0 and rows % 64 == 0 and rows * n % 512 == 0:
            return fused(n, mp_n, *arrays)
        return local(*arrays)

    return run


def solution(mesh):
    return jax.shard_map(
        choose(mesh),
        mesh=mesh,
        in_specs=(
            P(("dp", "seq"), "mp"),
            P(("dp", "seq", "mp"), None),
            P(("dp", "seq", "mp"), None),
            P(("dp", "seq", "mp"), None),
            P(("dp", "seq", "mp")),
            P("dp"),
            P(None, None, "mp"),
            P(None, "mp"),
        ),
        out_specs=(P(("dp", "seq"), "mp"), P(("dp", "seq"), "mp")),
        check_vma=False,
    )
```

```python
import functools

import jax
import jax.numpy as jnp
from jax import lax
from jax.experimental import pallas as pl
from jax.experimental.pallas import tpu as pltpu
from jax.sharding import PartitionSpec as P

HEAD_DIM = 128
VIDEOS = 4
MARK = 2.0**50
MESH = pl.DeviceIdType.MESH


def rows_at(index, count):
    return pl.ds(pl.multiple_of(index * count, count), count)


def whole(ref, sem):
    return pltpu.make_async_copy(ref, ref, sem)


def fused_kernel(
    n, mp_n,
    q_ref, k_ref, v_ref, ids_ref, step_ref, mod_ref, res_ref, w_ref,
    stream_ref, stat_out, mod_out,
    acc, qkv, key_marks, query_marks, values_t, obuf, att, wbuf, res, mods, ids_mine, counts,
    stat_mine, stat_other,
    qkv_send, qkv_recv, o_send, o_recv, fwd_send, fwd_recv,
    cnt_send, cnt_recv, stat_send, stat_recv, w_sem, in_sem, out_sem,
):
    seq_i = lax.axis_index("seq")
    mp_i = lax.axis_index("mp")
    me = seq_i * mp_n + mp_i
    rows = q_ref.shape[0]
    groups = qkv.shape[0]
    tokens = qkv.shape[2]
    columns = w_ref.shape[1]
    sibling = {"mp": 1 - mp_i}

    def device(p):
        return {"seq": lax.div(p, mp_n), "mp": lax.rem(p, mp_n)}

    x, y = lax.rem(seq_i, 2), lax.div(seq_i, 2)
    beside = y * 2 + 1 - x
    opposite = (1 - y) * 2 + x
    across = (1 - y) * 2 + 1 - x
    first = beside + mp_i * (opposite - beside)
    second = opposite + mp_i * (beside - opposite)
    peers_in_turn = [
        chip * mp_n + core
        for chip, core in (
            (first, mp_i), (second, 1 - mp_i), (across, mp_i),
            (first, 1 - mp_i), (second, mp_i), (across, 1 - mp_i),
            (seq_i, 1 - mp_i),
        )
    ]

    def each_peer(body):
        for p in peers_in_turn:
            body(p)

    def every(body):
        def step(p, carry):
            body(p)
            return carry

        lax.fori_loop(0, n, step, 0)

    def send_group(g):
        for t, ref in enumerate((k_ref, q_ref, v_ref)):

            def send(p, ref=ref, t=t):
                pltpu.make_async_remote_copy(
                    src_ref=ref.at[:, rows_at(p * groups + g, HEAD_DIM)],
                    dst_ref=qkv.at[g, t, rows_at(me, rows)],
                    send_sem=qkv_send.at[g],
                    recv_sem=qkv_recv.at[g],
                    device_id=device(p),
                    device_id_type=MESH,
                ).start()

            each_peer(send)
            pltpu.make_async_copy(
                ref.at[:, rows_at(me * groups + g, HEAD_DIM)],
                qkv.at[g, t, rows_at(me, rows)],
                qkv_recv.at[g],
            ).start()

    barrier = pltpu.get_barrier_semaphore()
    each_peer(
        lambda p: pl.semaphore_signal(
            barrier, inc=1, device_id=device(p), device_id_type=MESH
        )
    )
    load_ids = pltpu.make_async_copy(ids_ref, ids_mine, in_sem.at[0])
    load_res = pltpu.make_async_copy(res_ref, res, in_sem.at[1])
    load_mods = pltpu.make_async_copy(mod_ref, mods, in_sem.at[2])
    load_ids.start()
    pl.semaphore_wait(barrier, n - 1)

    ahead = 2
    for g in range(min(ahead, groups)):
        send_group(g)

    load_ids.wait()
    ids = ids_mine[...]
    below = [
        jnp.sum((ids <= k).astype(jnp.float32), axis=1, keepdims=True)
        for k in range(VIDEOS - 1)
    ]
    line = lax.broadcasted_iota(jnp.int32, (8, 128), 0)
    mine = jnp.where(line == 0, below[0], jnp.where(line == 1, below[1], below[2]))
    counts[rows_at(me, 8), :] = mine

    def send_count(p):
        pltpu.make_async_remote_copy(
            src_ref=counts.at[rows_at(me, 8)],
            dst_ref=counts.at[rows_at(me, 8)],
            send_sem=cnt_send,
            recv_sem=cnt_recv,
            device_id=device(p),
            device_id_type=MESH,
        ).start()

    each_peer(send_count)
    load_res.start()
    load_mods.start()
    for g in range(groups):

        def load_weight(p, g=g):
            pltpu.make_async_copy(
                w_ref.at[rows_at(p * groups + g, HEAD_DIM)],
                wbuf.at[g, rows_at(p, HEAD_DIM)],
                w_sem.at[g],
            ).start()

        every(load_weight)

    whole(counts.at[pl.ds(0, 8 * (n - 1))], cnt_recv).wait()
    sums = counts[pl.ds(0, 8), :]
    for r in range(1, n):
        sums = sums + counts[pl.ds(8 * r, 8), :]
    totals = [sums[k : k + 1, 0:1] for k in range(VIDEOS - 1)]
    tile = 2 * HEAD_DIM

    def mark(i, carry):
        at = rows_at(i, tile)
        place = (lax.broadcasted_iota(jnp.int32, (tile, 1), 0) + i * tile).astype(
            jnp.float32
        )
        own = sum((place >= c).astype(jnp.float32) for c in totals)
        video = lax.broadcasted_iota(jnp.int32, (tile, HEAD_DIM), 1).astype(jnp.float32)
        key_marks[at, :] = jnp.where(own == video, -MARK, 0.0).astype(jnp.bfloat16)
        other = jnp.where(own == video, 0.0, MARK)
        query_marks[at, :] = jnp.where(video < VIDEOS, other, 0.0).astype(jnp.bfloat16)
        return carry

    lax.fori_loop(0, tokens // tile, mark, 0)
    values_t[HEAD_DIM:, :] = jnp.ones((values_t.shape[0] - HEAD_DIM, tokens), jnp.bfloat16)
    chunk = tokens // 2
    peers = n // 2

    def attend_tile(g, start):
        at = pl.ds(pl.multiple_of(start, tile), tile)
        score = lax.dot_general(
            jnp.concatenate([qkv[g, 0], key_marks[...]], axis=1),
            jnp.concatenate([qkv[g, 1, at, :], query_marks[at, :]], axis=1),
            (((1,), (1,)), ((), ())),
            preferred_element_type=jnp.float32,
        )
        top = jnp.max(score, axis=0, keepdims=True)
        weight = jnp.exp((score - top) * (1.0 / HEAD_DIM**0.5)).astype(jnp.bfloat16)
        summed = jnp.dot(values_t[...], weight, preferred_element_type=jnp.float32)
        result = summed[:HEAD_DIM] / summed[HEAD_DIM : HEAD_DIM + 1]
        obuf[g, at, :] = result.T.astype(jnp.bfloat16)

    def attend_and_send(g):
        values_t[:HEAD_DIM, :] = qkv[g, 2].T

        def half(j, carry):
            part = lax.rem(lax.div(me, peers) + 1 + j, 2)
            for i in range(chunk // tile):
                attend_tile(g, part * chunk + i * tile)

            def send(d, carry):
                p = part * peers + lax.rem(me + d, peers)
                block = obuf.at[g, rows_at(p, rows)]
                there = att.at[
                    g, rows_at(lax.rem(p, mp_n), rows), rows_at(me, HEAD_DIM)
                ]

                @pl.when(p != me)
                def _():
                    pltpu.make_async_remote_copy(
                        src_ref=block,
                        dst_ref=there,
                        send_sem=o_send.at[g],
                        recv_sem=o_recv.at[g, me],
                        device_id=device(p),
                        device_id_type=MESH,
                    ).start()

                @pl.when(p == me)
                def _():
                    pltpu.make_async_copy(block, there, o_recv.at[g, me]).start()

                return carry

            return lax.fori_loop(0, peers, send, carry)

        lax.fori_loop(0, 2, half, 0)

    def pass_on(g):
        def step(d, carry):
            p = lax.rem(me + n - d, n)
            block = att.at[g, rows_at(mp_i, rows), rows_at(p, HEAD_DIM)]
            whole(block, o_recv.at[g, p]).wait()
            pltpu.make_async_remote_copy(
                src_ref=block,
                dst_ref=block,
                send_sem=fwd_send.at[g],
                recv_sem=fwd_recv.at[g],
                device_id=sibling,
                device_id_type=MESH,
            ).start()
            return carry

        lax.fori_loop(1, n + 1, step, 0)

    def project(g, half):
        rows_of = rows_at(half, rows)
        tile = 2 * HEAD_DIM

        def step(i, carry):
            at = rows_at(i, tile)
            part = jnp.dot(
                att[g, rows_of, :], wbuf[g, :, at], preferred_element_type=jnp.float32
            )
            acc[rows_of, at] = part if g == 0 else acc[rows_of, at] + part
            return carry

        lax.fori_loop(0, columns // tile, step, 0)

    def wait_forward(g):
        whole(att.at[g, rows_at(1 - mp_i, rows)], fwd_recv.at[g]).wait()

    def project_both(g):
        whole(wbuf.at[g], w_sem.at[g]).wait()
        wait_forward(g)
        project(g, mp_i)
        project(g, 1 - mp_i)

    for g in range(groups):
        whole(qkv.at[g], qkv_recv.at[g]).wait()
        if g + ahead < groups:
            send_group(g + ahead)
        attend_and_send(g)
        if g >= 1:
            pass_on(g - 1)
        if g >= 2:
            project_both(g - 2)
    if groups >= 2:
        project_both(groups - 2)
    last = groups - 1
    pass_on(last)

    load_res.wait()
    load_mods.wait()
    chosen = step_ref[0]
    gate = mods[0, pl.ds(chosen, 1), :]
    mod_out[0:1, :] = mods[1, pl.ds(chosen, 1), :]
    mod_out[1:2, :] = mods[2, pl.ds(chosen, 1), :]
    tile = rows // 3 if rows % 48 == 0 else 16
    side = lax.broadcasted_iota(jnp.int32, (tile, 128), 1) < 64

    def stats(half):
        part = rows_at(half, rows)
        return pltpu.make_async_remote_copy(
            src_ref=stat_mine.at[part],
            dst_ref=stat_other.at[part],
            send_sem=stat_send.at[half],
            recv_sem=stat_recv.at[half],
            device_id=sibling,
            device_id_type=MESH,
        )

    def store(half):
        part = rows_at(half, rows)
        return pltpu.make_async_copy(acc.at[part], stream_ref.at[part], out_sem.at[half])

    def finish(half):
        project(last, half)

        def gated(i, carry):
            at = rows_at(half * (rows // tile) + i, tile)
            stream = res[at, :].astype(jnp.float32) + gate * acc[at, :]
            acc[at, :] = stream
            row_sum = jnp.sum(stream, axis=1, keepdims=True)
            row_sq = jnp.sum(stream * stream, axis=1, keepdims=True)
            stat_mine[at, :] = jnp.where(side, row_sum, row_sq)
            return carry

        lax.fori_loop(0, rows // tile, gated, 0)
        stats(half).start()
        store(half).start()

    whole(wbuf.at[last], w_sem.at[last]).wait()
    finish(mp_i)
    wait_forward(last)
    finish(1 - mp_i)

    whole(counts.at[pl.ds(0, 8 * (n - 1))], cnt_send).wait()
    for g in range(groups):
        whole(qkv.at[g, :, pl.ds(0, rows * (n - 1))], qkv_send.at[g]).wait()
        whole(obuf.at[g, pl.ds(0, rows * (n - 1))], o_send.at[g]).wait()
        whole(att.at[g, rows_at(mp_i, rows)], fwd_send.at[g]).wait()
    for half in range(2):
        stats(half).wait_recv()
    stat_out[...] = stat_mine[...] + stat_other[...]
    for half in range(2):
        stats(half).wait_send()
        store(half).wait()


def norm_kernel(
    width, stream_ref, stat_ref, mod_ref, hid_ref, mlp_ref,
    stream_in, stat, mod, hid, mlp, load_sems, sems,
):
    tile = 64
    count = stream_ref.shape[0] // tile
    load_mod = pltpu.make_async_copy(mod_ref, mod, load_sems.at[count])
    load_stat = pltpu.make_async_copy(stat_ref, stat, load_sems.at[count + 1])
    load_mod.start()
    load_stat.start()
    loads = []
    for i in range(count):
        at = pl.ds(i * tile, tile)
        loads.append(
            pltpu.make_async_copy(stream_ref.at[at], stream_in.at[at], load_sems.at[i])
        )
        loads[i].start()
    load_mod.wait()
    load_stat.wait()
    shift = mod[0:1, :]
    scale = 1.0 + mod[1:2, :]
    copies = []
    for i in range(count):
        at = pl.ds(i * tile, tile)
        loads[i].wait()
        stream = stream_in[at, :]
        mean = stat[at, 0:1] / width
        var = stat[at, 64:65] / width - mean * mean
        hid[at, :] = stream.astype(jnp.bfloat16)
        result = (stream - mean) * lax.rsqrt(var + 1e-06) * scale + shift
        mlp[at, :] = result.astype(jnp.bfloat16)
        for k, (source, target) in enumerate(((hid, hid_ref), (mlp, mlp_ref))):
            copy = pltpu.make_async_copy(source.at[at], target.at[at], sems.at[k, i])
            copy.start()
            copies.append(copy)
    for copy in copies:
        copy.wait()


def fused(n, mp_n, residual, queries, keys, values, video_ids, timestep, modulation, out_weight):
    rows, width = queries.shape
    high, columns = residual.shape
    tokens = rows * n
    groups = width // HEAD_DIM // n
    steps = modulation.shape[0]
    bf16, f32 = jnp.bfloat16, jnp.float32
    dma = pltpu.SemaphoreType.DMA
    hbm = pl.BlockSpec(memory_space=pltpu.HBM)
    smem = pl.BlockSpec(memory_space=pltpu.SMEM)
    vmem = pl.BlockSpec(memory_space=pltpu.VMEM)
    stream, stat, mods = pl.pallas_call(
        functools.partial(fused_kernel, n, mp_n),
        out_shape=(
            jax.ShapeDtypeStruct((high, columns), f32),
            jax.ShapeDtypeStruct((high, 128), f32),
            jax.ShapeDtypeStruct((2, columns), f32),
        ),
        in_specs=[hbm, hbm, hbm, hbm, smem, hbm, hbm, hbm],
        out_specs=(hbm, vmem, vmem),
        scratch_shapes=[
            pltpu.VMEM((high, columns), f32),
            pltpu.VMEM((groups, 3, tokens, HEAD_DIM), bf16),
            pltpu.VMEM((tokens, HEAD_DIM), bf16),
            pltpu.VMEM((tokens, HEAD_DIM), bf16),
            pltpu.VMEM((HEAD_DIM + 16, tokens), bf16),
            pltpu.VMEM((groups, tokens, HEAD_DIM), bf16),
            pltpu.VMEM((groups, high, n * HEAD_DIM), bf16),
            pltpu.VMEM((groups, n * HEAD_DIM, columns), bf16),
            pltpu.VMEM((high, columns), bf16),
            pltpu.VMEM((3, steps, columns), f32),
            pltpu.VMEM((1, rows), jnp.int32),
            pltpu.VMEM((8 * n, 128), f32),
            pltpu.VMEM((high, 128), f32),
            pltpu.VMEM((high, 128), f32),
            dma((groups,)), dma((groups,)),
            dma((groups,)), dma((groups, n)), dma((groups,)), dma((groups,)),
            dma, dma, dma((2,)), dma((2,)), dma((groups,)), dma((3,)),
            dma((2,)),
        ],
        compiler_params=pltpu.CompilerParams(
            collective_id=0, has_side_effects=True, vmem_limit_bytes=56 * 2**20
        ),
    )(
        queries, keys, values, video_ids.reshape(1, rows), timestep,
        modulation.transpose(1, 0, 2), residual, out_weight,
    )
    out = jax.ShapeDtypeStruct(residual.shape, bf16)
    return pl.pallas_call(
        functools.partial(norm_kernel, width),
        out_shape=(out, out),
        in_specs=[hbm, hbm, hbm],
        out_specs=(hbm, hbm),
        scratch_shapes=[
            pltpu.VMEM((high, columns), f32),
            pltpu.VMEM((high, 128), f32),
            pltpu.VMEM((2, columns), f32),
            pltpu.VMEM((high, columns), bf16),
            pltpu.VMEM((high, columns), bf16),
            dma((high // 64 + 2,)),
            dma((2, high // 64)),
        ],
        compiler_params=pltpu.CompilerParams(vmem_limit_bytes=56 * 2**20),
    )(stream, stat, mods)


def attend(carry, q_rows, q_ids, key_rows, value_rows, key_ids):
    top, total, summed = carry
    rows = q_rows.shape[0]
    count = key_rows.shape[0]
    heads = q_rows.shape[1] // HEAD_DIM
    factor = 1.0 / HEAD_DIM**0.5
    q_heads = q_rows.reshape(rows, heads, HEAD_DIM)
    k_heads = key_rows.reshape(count, heads, HEAD_DIM)
    v_heads = value_rows.reshape(count, heads, HEAD_DIM)
    same = (q_ids[:, None] == key_ids[None, :])[None]
    new_top, new_total, new_summed = ([], [], [])
    for first in range(0, heads, 3):
        score = (
            jnp.einsum(
                "thd,nhd->htn",
                q_heads[:, first : first + 3],
                k_heads[:, first : first + 3],
                preferred_element_type=jnp.float32,
            )
            * factor
        )
        score = jnp.where(same, score, -1e30)
        old_top = top[first : first + 3]
        peak = jnp.maximum(old_top, jnp.max(score, axis=2))
        weight = jnp.where(same, jnp.exp(score - peak[:, :, None]), 0.0)
        new_top.append(peak)
        new_total.append(jnp.sum(weight, axis=2))
        part_sum = jnp.einsum(
            "htn,nhd->htd",
            weight.astype(jnp.bfloat16),
            v_heads[:, first : first + 3],
            preferred_element_type=jnp.float32,
        )
        new_summed.append(part_sum)
    return (
        jnp.concatenate(new_top, 0),
        jnp.concatenate(new_total, 0),
        jnp.concatenate(new_summed, 0),
    )


def attend_maybe(carry, q_rows, q_ids, key_rows, value_rows, key_ids):
    return attend(carry, q_rows, q_ids, key_rows, value_rows, key_ids)


def start_state(q_rows):
    rows = q_rows.shape[0]
    heads = q_rows.shape[1] // HEAD_DIM
    return (
        jnp.full((heads, rows), -1e30, jnp.float32),
        jnp.zeros((heads, rows), jnp.float32),
        jnp.zeros((heads, rows, HEAD_DIM), jnp.float32),
    )


def finish(state, q_rows):
    top, total, summed = state
    rows = q_rows.shape[0]
    heads = q_rows.shape[1] // HEAD_DIM
    result = summed / total[:, :, None]
    return result.transpose(1, 0, 2).reshape(rows, heads * HEAD_DIM).astype(jnp.bfloat16)


def local(residual, queries, keys, values, video_ids, timestep, modulation, out_weight):
    steps_count = modulation.shape[0]
    picker = (jnp.arange(steps_count, dtype=jnp.int32) == timestep[0]).astype(jnp.float32)
    mod_rows = jnp.einsum("s,scd->cd", picker, modulation, precision=lax.Precision.HIGHEST)
    gate = mod_rows[0]
    shift = mod_rows[1]
    scale = mod_rows[2]
    width = queries.shape[1]
    state = attend_maybe(
        start_state(queries),
        queries,
        video_ids,
        lax.all_gather(keys, ("seq", "mp"), axis=0, tiled=True),
        lax.all_gather(values, ("seq", "mp"), axis=0, tiled=True),
        lax.all_gather(video_ids, ("seq", "mp"), axis=0, tiled=True),
    )
    attended = finish(state, queries)
    projected = jnp.dot(
        lax.all_gather(attended, "mp", axis=0, tiled=True),
        out_weight,
        preferred_element_type=jnp.float32,
    )
    stream = residual.astype(jnp.float32) + gate[None, :] * projected
    row_sum = jnp.sum(stream, axis=1, keepdims=True)
    row_sq = jnp.sum(stream * stream, axis=1, keepdims=True)
    row_sum, row_sq = lax.psum((row_sum, row_sq), "mp")
    mean = row_sum / width
    var = row_sq / width - mean * mean
    normed = (stream - mean) * lax.rsqrt(var + 1e-06) * (1.0 + scale[None, :]) + shift[None, :]
    return (stream.astype(jnp.bfloat16), normed.astype(jnp.bfloat16))


def choose(mesh):
    seq_n, mp_n = mesh.shape["seq"], mesh.shape["mp"]
    n = seq_n * mp_n

    def run(*arrays):
        queries = arrays[1]
        rows, width = queries.shape
        if mp_n == 2 and seq_n == 4 and width // HEAD_DIM % n == 0 and rows % 64 == 0 and rows * n % 512 == 0:
            return fused(n, mp_n, *arrays)
        return local(*arrays)

    return run


def solution(mesh):
    return jax.shard_map(
        choose(mesh),
        mesh=mesh,
        in_specs=(
            P(("dp", "seq"), "mp"),
            P(("dp", "seq", "mp"), None),
            P(("dp", "seq", "mp"), None),
            P(("dp", "seq", "mp"), None),
            P(("dp", "seq", "mp")),
            P("dp"),
            P(None, None, "mp"),
            P(None, "mp"),
        ),
        out_specs=(P(("dp", "seq"), "mp"), P(("dp", "seq"), "mp")),
        check_vma=False,
    )
```

```python
import functools
import math

import jax
import jax.numpy as jnp
from jax import lax
from jax.experimental import pallas as pl
from jax.experimental.pallas import tpu as pltpu
from jax.sharding import PartitionSpec as P

HEAD_DIM = 128
VIDEOS = 4
MESH = pl.DeviceIdType.MESH


def rows_at(index, count):
    return pl.ds(pl.multiple_of(index * count, count), count)


def whole(ref, sem):
    return pltpu.make_async_copy(ref, ref, sem)


def fused_kernel(
    n, mp_n, width,
    q_ref, k_ref, v_ref, ids_ref, mod_ref, res_ref, w_ref,
    hid_ref, mlp_ref,
    qkv, obuf, att, wbuf, res, acc, hid, mlp, counts, stat_mine, stat_other,
    qkv_send, qkv_recv, o_send, o_recv, fwd_send, fwd_recv,
    cnt_send, cnt_recv, stat_send, stat_recv, w_sem, res_sem, out_sem,
):
    seq_i = lax.axis_index("seq")
    mp_i = lax.axis_index("mp")
    me = seq_i * mp_n + mp_i
    rows = q_ref.shape[0]
    groups = qkv.shape[0]
    tokens = qkv.shape[2]
    columns = w_ref.shape[1]
    sibling = {"mp": 1 - mp_i}

    def device(p):
        return {"seq": lax.div(p, mp_n), "mp": lax.rem(p, mp_n)}

    def each_peer(body):
        def step(d, carry):
            body(lax.rem(me + d, n))
            return carry

        lax.fori_loop(1, n, step, 0)

    def load_weight(g, p):
        return pltpu.make_async_copy(
            w_ref.at[rows_at(p * groups + g, HEAD_DIM)],
            wbuf.at[g, rows_at(p, HEAD_DIM)],
            w_sem.at[g],
        )

    load_res = pltpu.make_async_copy(res_ref, res, res_sem)

    ids = ids_ref[...]
    below = [
        jnp.sum((ids <= k).astype(jnp.float32), axis=1, keepdims=True)
        for k in range(VIDEOS - 1)
    ]
    line = lax.broadcasted_iota(jnp.int32, (8, 128), 0)
    mine = jnp.where(line == 0, below[0], jnp.where(line == 1, below[1], below[2]))
    counts[rows_at(me, 8), :] = mine

    barrier = pltpu.get_barrier_semaphore()
    each_peer(
        lambda p: pl.semaphore_signal(
            barrier, inc=1, device_id=device(p), device_id_type=MESH
        )
    )
    pl.semaphore_wait(barrier, n - 1)

    def send_count(p):
        pltpu.make_async_remote_copy(
            src_ref=counts.at[rows_at(me, 8)],
            dst_ref=counts.at[rows_at(me, 8)],
            send_sem=cnt_send,
            recv_sem=cnt_recv,
            device_id=device(p),
            device_id_type=MESH,
        ).start()

    each_peer(send_count)

    def send_group(g):
        for t, ref in enumerate((k_ref, q_ref, v_ref)):

            def send(p, ref=ref, t=t):
                pltpu.make_async_remote_copy(
                    src_ref=ref.at[:, rows_at(p * groups + g, HEAD_DIM)],
                    dst_ref=qkv.at[g, t, rows_at(me, rows)],
                    send_sem=qkv_send.at[g],
                    recv_sem=qkv_recv.at[g],
                    device_id=device(p),
                    device_id_type=MESH,
                ).start()

            each_peer(send)
            pltpu.make_async_copy(
                ref.at[:, rows_at(me * groups + g, HEAD_DIM)],
                qkv.at[g, t, rows_at(me, rows)],
                qkv_recv.at[g],
            ).start()

    def attention(g, totals):
        lane = lax.broadcasted_iota(jnp.int32, (1, tokens), 1).astype(jnp.float32)
        key_ids = sum((lane >= c).astype(jnp.float32) for c in totals)
        tile = 2 * HEAD_DIM
        factor = math.log2(math.e) / HEAD_DIM**0.5

        reach = tokens // 2
        for first in range(0, tokens, tile):
            at = pl.ds(first, tile)
            low = max(0, first - reach)
            high = min(tokens, first + tile + reach)
            near = pl.ds(low, high - low)
            place = (lax.broadcasted_iota(jnp.int32, (tile, 1), 0) + first).astype(
                jnp.float32
            )
            own_ids = sum((place >= c).astype(jnp.float32) for c in totals)
            score = lax.dot_general(
                qkv[g, 1, at, :],
                qkv[g, 0, near, :],
                (((1,), (1,)), ((), ())),
                preferred_element_type=jnp.float32,
            )
            score = jnp.where(own_ids == key_ids[:, low:high], score, -1e30)
            top = jnp.max(score, axis=1, keepdims=True)
            weight = jnp.exp2((score - top) * factor)
            total = jnp.sum(weight, axis=1, keepdims=True)
            summed = jnp.dot(
                weight.astype(jnp.bfloat16),
                qkv[g, 2, near, :],
                preferred_element_type=jnp.float32,
            )
            obuf[g, at, :] = (summed / total).astype(jnp.bfloat16)

    def send_back(g):
        def send(p):
            pltpu.make_async_remote_copy(
                src_ref=obuf.at[g, rows_at(p, rows)],
                dst_ref=att.at[
                    g, rows_at(lax.rem(p, mp_n), rows), rows_at(me, HEAD_DIM)
                ],
                send_sem=o_send.at[g],
                recv_sem=o_recv.at[g],
                device_id=device(p),
                device_id_type=MESH,
            ).start()

        each_peer(send)
        pltpu.make_async_copy(
            obuf.at[g, rows_at(me, rows)],
            att.at[g, rows_at(mp_i, rows), rows_at(me, HEAD_DIM)],
            o_recv.at[g],
        ).start()

    def forward(g):
        half = att.at[g, rows_at(mp_i, rows)]
        return pltpu.make_async_remote_copy(
            src_ref=half,
            dst_ref=half,
            send_sem=fwd_send.at[g],
            recv_sem=fwd_recv.at[g],
            device_id=sibling,
            device_id_type=MESH,
        )

    def pass_on(g):
        whole(att.at[g, rows_at(mp_i, rows)], o_recv.at[g]).wait()
        forward(g).start()

    def project(g):
        whole(wbuf.at[g], w_sem.at[g]).wait()
        whole(att.at[g, rows_at(1 - mp_i, rows)], fwd_recv.at[g]).wait()
        tile = 2 * HEAD_DIM

        def step(i, carry):
            at = rows_at(i, tile)
            part = jnp.dot(
                att[g], wbuf[g, :, at], preferred_element_type=jnp.float32
            )
            acc[:, at] += part
            return carry

        lax.fori_loop(0, columns // tile, step, 0)

    send_group(0)
    if groups > 1:
        send_group(1)
    load_res.start()
    for g in range(groups):

        def start_load(p, carry, g=g):
            load_weight(g, p).start()
            return carry

        lax.fori_loop(0, n, start_load, 0)
    whole(counts.at[pl.ds(0, 8 * (n - 1))], cnt_recv).wait()
    sums = counts[pl.ds(0, 8), :]
    for r in range(1, n):
        sums = sums + counts[pl.ds(8 * r, 8), :]
    totals = [sums[k : k + 1, 0:1] for k in range(VIDEOS - 1)]

    acc[...] = jnp.zeros_like(acc)

    def group(g, carry):
        whole(qkv.at[g], qkv_recv.at[g]).wait()

        @pl.when(g + 2 < groups)
        def _():
            send_group(g + 2)

        attention(g, totals)
        send_back(g)

        @pl.when(g >= 1)
        def _():
            pass_on(g - 1)

        @pl.when(g >= 2)
        def _():
            project(g - 2)

        return carry

    lax.fori_loop(0, groups, group, 0)
    if groups >= 2:
        project(groups - 2)
    pass_on(groups - 1)
    project(groups - 1)

    load_res.wait()
    gate = mod_ref[0:1, :]
    shift = mod_ref[1:2, :]
    scale = 1.0 + mod_ref[2:3, :]
    high = acc.shape[0]
    tile = 64
    side = lax.broadcasted_iota(jnp.int32, (tile, 128), 1) < 64

    def gated(i, carry):
        at = rows_at(i, tile)
        stream = res[at, :].astype(jnp.float32) + gate * acc[at, :]
        acc[at, :] = stream
        hid[at, :] = stream.astype(jnp.bfloat16)
        row_sum = jnp.sum(stream, axis=1, keepdims=True)
        row_sq = jnp.sum(stream * stream, axis=1, keepdims=True)
        stat_mine[at, :] = jnp.where(side, row_sum, row_sq)
        return carry

    lax.fori_loop(0, high // tile, gated, 0)
    stats = pltpu.make_async_remote_copy(
        src_ref=stat_mine,
        dst_ref=stat_other,
        send_sem=stat_send,
        recv_sem=stat_recv,
        device_id=sibling,
        device_id_type=MESH,
    )
    stats.start()
    store_hid = pltpu.make_async_copy(hid, hid_ref, out_sem.at[0])
    store_hid.start()
    stats.wait_recv()

    def normed(i, carry):
        at = rows_at(i, tile)
        both = stat_mine[at, :] + stat_other[at, :]
        mean = both[:, 0:1] / width
        var = both[:, 64:65] / width - mean * mean
        stream = acc[at, :]
        result = (stream - mean) * lax.rsqrt(var + 1e-06) * scale + shift
        mlp[at, :] = result.astype(jnp.bfloat16)
        return carry

    lax.fori_loop(0, high // tile, normed, 0)
    store_mlp = pltpu.make_async_copy(mlp, mlp_ref, out_sem.at[1])
    store_mlp.start()

    stats.wait_send()
    whole(counts.at[pl.ds(0, 8 * (n - 1))], cnt_send).wait()
    for g in range(groups):
        whole(qkv.at[g, :, pl.ds(0, rows * (n - 1))], qkv_send.at[g]).wait()
        whole(obuf.at[g, pl.ds(0, rows * (n - 1))], o_send.at[g]).wait()
        forward(g).wait_send()
    store_hid.wait()
    store_mlp.wait()


def fused(n, mp_n, residual, queries, keys, values, video_ids, timestep, modulation, out_weight):
    mod_rows = lax.dynamic_index_in_dim(modulation, timestep[0], 0, keepdims=False)
    rows, width = queries.shape
    high, columns = residual.shape
    tokens = rows * n
    groups = width // HEAD_DIM // n
    bf16 = jnp.bfloat16
    dma = pltpu.SemaphoreType.DMA
    anywhere = pl.BlockSpec(memory_space=pl.ANY)
    vmem = pl.BlockSpec(memory_space=pltpu.VMEM)
    out = jax.ShapeDtypeStruct(residual.shape, bf16)
    return pl.pallas_call(
        functools.partial(fused_kernel, n, mp_n, width),
        out_shape=(out, out),
        in_specs=[anywhere, anywhere, anywhere, vmem, vmem, anywhere, anywhere],
        out_specs=(anywhere, anywhere),
        scratch_shapes=[
            pltpu.VMEM((groups, 3, tokens, HEAD_DIM), bf16),
            pltpu.VMEM((groups, tokens, HEAD_DIM), bf16),
            pltpu.VMEM((groups, high, n * HEAD_DIM), bf16),
            pltpu.VMEM((groups, n * HEAD_DIM, columns), bf16),
            pltpu.VMEM((high, columns), bf16),
            pltpu.VMEM((high, columns), jnp.float32),
            pltpu.VMEM((high, columns), bf16),
            pltpu.VMEM((high, columns), bf16),
            pltpu.VMEM((8 * n, 128), jnp.float32),
            pltpu.VMEM((high, 128), jnp.float32),
            pltpu.VMEM((high, 128), jnp.float32),
            dma((groups,)), dma((groups,)), dma((groups,)), dma((groups,)),
            dma((groups,)), dma((groups,)),
            dma, dma, dma, dma, dma((groups,)), dma, dma((2,)),
        ],
        compiler_params=pltpu.CompilerParams(
            collective_id=0, has_side_effects=True, vmem_limit_bytes=52 * 2**20
        ),
    )(queries, keys, values, video_ids.reshape(1, rows), mod_rows, residual, out_weight)


def attend(carry, q_rows, q_ids, key_rows, value_rows, key_ids):
    top, total, summed = carry
    rows = q_rows.shape[0]
    count = key_rows.shape[0]
    heads = q_rows.shape[1] // HEAD_DIM
    factor = 1.0 / HEAD_DIM**0.5
    q_heads = q_rows.reshape(rows, heads, HEAD_DIM)
    k_heads = key_rows.reshape(count, heads, HEAD_DIM)
    v_heads = value_rows.reshape(count, heads, HEAD_DIM)
    same = (q_ids[:, None] == key_ids[None, :])[None]
    new_top, new_total, new_summed = ([], [], [])
    for first in range(0, heads, 3):
        score = (
            jnp.einsum(
                "thd,nhd->htn",
                q_heads[:, first : first + 3],
                k_heads[:, first : first + 3],
                preferred_element_type=jnp.float32,
            )
            * factor
        )
        score = jnp.where(same, score, -1e30)
        old_top = top[first : first + 3]
        peak = jnp.maximum(old_top, jnp.max(score, axis=2))
        weight = jnp.where(same, jnp.exp(score - peak[:, :, None]), 0.0)
        new_top.append(peak)
        new_total.append(jnp.sum(weight, axis=2))
        part_sum = jnp.einsum(
            "htn,nhd->htd",
            weight.astype(jnp.bfloat16),
            v_heads[:, first : first + 3],
            preferred_element_type=jnp.float32,
        )
        new_summed.append(part_sum)
    return (
        jnp.concatenate(new_top, 0),
        jnp.concatenate(new_total, 0),
        jnp.concatenate(new_summed, 0),
    )


def attend_maybe(carry, q_rows, q_ids, key_rows, value_rows, key_ids):
    return attend(carry, q_rows, q_ids, key_rows, value_rows, key_ids)


def start_state(q_rows):
    rows = q_rows.shape[0]
    heads = q_rows.shape[1] // HEAD_DIM
    return (
        jnp.full((heads, rows), -1e30, jnp.float32),
        jnp.zeros((heads, rows), jnp.float32),
        jnp.zeros((heads, rows, HEAD_DIM), jnp.float32),
    )


def finish(state, q_rows):
    top, total, summed = state
    rows = q_rows.shape[0]
    heads = q_rows.shape[1] // HEAD_DIM
    result = summed / total[:, :, None]
    return result.transpose(1, 0, 2).reshape(rows, heads * HEAD_DIM).astype(jnp.bfloat16)


def local(residual, queries, keys, values, video_ids, timestep, modulation, out_weight):
    steps_count = modulation.shape[0]
    picker = (jnp.arange(steps_count, dtype=jnp.int32) == timestep[0]).astype(jnp.float32)
    mod_rows = jnp.einsum("s,scd->cd", picker, modulation, precision=lax.Precision.HIGHEST)
    gate = mod_rows[0]
    shift = mod_rows[1]
    scale = mod_rows[2]
    width = queries.shape[1]
    state = attend_maybe(
        start_state(queries),
        queries,
        video_ids,
        lax.all_gather(keys, ("seq", "mp"), axis=0, tiled=True),
        lax.all_gather(values, ("seq", "mp"), axis=0, tiled=True),
        lax.all_gather(video_ids, ("seq", "mp"), axis=0, tiled=True),
    )
    attended = finish(state, queries)
    projected = jnp.dot(
        lax.all_gather(attended, "mp", axis=0, tiled=True),
        out_weight,
        preferred_element_type=jnp.float32,
    )
    stream = residual.astype(jnp.float32) + gate[None, :] * projected
    row_sum = jnp.sum(stream, axis=1, keepdims=True)
    row_sq = jnp.sum(stream * stream, axis=1, keepdims=True)
    row_sum, row_sq = lax.psum((row_sum, row_sq), "mp")
    mean = row_sum / width
    var = row_sq / width - mean * mean
    normed = (stream - mean) * lax.rsqrt(var + 1e-06) * (1.0 + scale[None, :]) + shift[None, :]
    return (stream.astype(jnp.bfloat16), normed.astype(jnp.bfloat16))


def choose(mesh):
    seq_n, mp_n = mesh.shape["seq"], mesh.shape["mp"]
    n = seq_n * mp_n

    def run(*arrays):
        queries = arrays[1]
        rows, width = queries.shape
        if mp_n == 2 and width // HEAD_DIM % n == 0 and rows % 64 == 0 and rows * n % 256 == 0:
            return fused(n, mp_n, *arrays)
        return local(*arrays)

    return run


def solution(mesh):
    return jax.shard_map(
        choose(mesh),
        mesh=mesh,
        in_specs=(
            P(("dp", "seq"), "mp"),
            P(("dp", "seq", "mp"), None),
            P(("dp", "seq", "mp"), None),
            P(("dp", "seq", "mp"), None),
            P(("dp", "seq", "mp")),
            P("dp"),
            P(None, None, "mp"),
            P(None, "mp"),
        ),
        out_specs=(P(("dp", "seq"), "mp"), P(("dp", "seq"), "mp")),
        check_vma=False,
    )
```

```python
import functools
import math

import jax
import jax.numpy as jnp
from jax import lax
from jax.experimental import pallas as pl
from jax.experimental.pallas import tpu as pltpu
from jax.sharding import PartitionSpec as P

HEAD_DIM = 128
VIDEOS = 4
MESH = pl.DeviceIdType.MESH


def rows_at(index, count):
    return pl.ds(pl.multiple_of(index * count, count), count)


def whole(ref, sem):
    return pltpu.make_async_copy(ref, ref, sem)


def fused_kernel(
    n, mp_n, width,
    q_ref, k_ref, v_ref, ids_ref, mod_ref, res_ref, w_ref,
    hid_ref, mlp_ref,
    qkv, obuf, att, wbuf, res, acc, hid, mlp, counts, stat_mine, stat_other,
    qkv_send, qkv_recv, o_send, o_recv, fwd_send, fwd_recv,
    cnt_send, cnt_recv, stat_send, stat_recv, w_sem, res_sem, out_sem,
):
    seq_i = lax.axis_index("seq")
    mp_i = lax.axis_index("mp")
    me = seq_i * mp_n + mp_i
    rows = q_ref.shape[0]
    groups = qkv.shape[0]
    tokens = qkv.shape[2]
    columns = w_ref.shape[1]
    sibling = {"mp": 1 - mp_i}

    def device(p):
        return {"seq": lax.div(p, mp_n), "mp": lax.rem(p, mp_n)}

    def each_peer(body):
        def step(d, carry):
            body(lax.rem(me + d, n))
            return carry

        lax.fori_loop(1, n, step, 0)

    def load_weight(g, p):
        return pltpu.make_async_copy(
            w_ref.at[rows_at(p * groups + g, HEAD_DIM)],
            wbuf.at[g, rows_at(p, HEAD_DIM)],
            w_sem.at[g],
        )

    load_res = pltpu.make_async_copy(res_ref, res, res_sem)

    ids = ids_ref[...]
    below = [
        jnp.sum((ids <= k).astype(jnp.float32), axis=1, keepdims=True)
        for k in range(VIDEOS - 1)
    ]
    line = lax.broadcasted_iota(jnp.int32, (8, 128), 0)
    mine = jnp.where(line == 0, below[0], jnp.where(line == 1, below[1], below[2]))
    counts[rows_at(me, 8), :] = mine

    barrier = pltpu.get_barrier_semaphore()
    each_peer(
        lambda p: pl.semaphore_signal(
            barrier, inc=1, device_id=device(p), device_id_type=MESH
        )
    )
    pl.semaphore_wait(barrier, n - 1)

    def send_count(p):
        pltpu.make_async_remote_copy(
            src_ref=counts.at[rows_at(me, 8)],
            dst_ref=counts.at[rows_at(me, 8)],
            send_sem=cnt_send,
            recv_sem=cnt_recv,
            device_id=device(p),
            device_id_type=MESH,
        ).start()

    each_peer(send_count)

    def send_group(g):
        for t, ref in enumerate((k_ref, q_ref, v_ref)):

            def send(p, ref=ref, t=t):
                pltpu.make_async_remote_copy(
                    src_ref=ref.at[:, rows_at(p * groups + g, HEAD_DIM)],
                    dst_ref=qkv.at[g, t, rows_at(me, rows)],
                    send_sem=qkv_send.at[g],
                    recv_sem=qkv_recv.at[g],
                    device_id=device(p),
                    device_id_type=MESH,
                ).start()

            each_peer(send)
            pltpu.make_async_copy(
                ref.at[:, rows_at(me * groups + g, HEAD_DIM)],
                qkv.at[g, t, rows_at(me, rows)],
                qkv_recv.at[g],
            ).start()

    def attention(g, totals, part):
        lane = lax.broadcasted_iota(jnp.int32, (1, tokens), 1).astype(jnp.float32)
        key_ids = sum((lane >= c).astype(jnp.float32) for c in totals)
        tile = 2 * HEAD_DIM
        factor = math.log2(math.e) / HEAD_DIM**0.5

        reach = tokens // 2
        for first in range(part * reach, (part + 1) * reach, tile):
            at = pl.ds(first, tile)
            low = max(0, first - reach)
            high = min(tokens, first + tile + reach)
            near = pl.ds(low, high - low)
            place = (lax.broadcasted_iota(jnp.int32, (tile, 1), 0) + first).astype(
                jnp.float32
            )
            own_ids = sum((place >= c).astype(jnp.float32) for c in totals)
            score = lax.dot_general(
                qkv[g, 1, at, :],
                qkv[g, 0, near, :],
                (((1,), (1,)), ((), ())),
                preferred_element_type=jnp.float32,
            )
            score = jnp.where(own_ids == key_ids[:, low:high], score, -1e30)
            top = jnp.max(score, axis=1, keepdims=True)
            weight = jnp.exp2((score - top) * factor)
            total = jnp.sum(weight, axis=1, keepdims=True)
            summed = jnp.dot(
                weight.astype(jnp.bfloat16),
                qkv[g, 2, near, :],
                preferred_element_type=jnp.float32,
            )
            obuf[g, at, :] = (summed / total).astype(jnp.bfloat16)

    def send_back(g, part):
        half = n // 2

        def send(d, carry):
            p = part * half + lax.rem(me + d, half)
            block = obuf.at[g, rows_at(p, rows)]
            there = att.at[g, rows_at(lax.rem(p, mp_n), rows), rows_at(me, HEAD_DIM)]

            @pl.when(p != me)
            def _():
                pltpu.make_async_remote_copy(
                    src_ref=block,
                    dst_ref=there,
                    send_sem=o_send.at[g],
                    recv_sem=o_recv.at[g],
                    device_id=device(p),
                    device_id_type=MESH,
                ).start()

            @pl.when(p == me)
            def _():
                pltpu.make_async_copy(block, there, o_recv.at[g]).start()

            return carry

        lax.fori_loop(0, half, send, 0)

    def forward(g):
        half = att.at[g, rows_at(mp_i, rows)]
        return pltpu.make_async_remote_copy(
            src_ref=half,
            dst_ref=half,
            send_sem=fwd_send.at[g],
            recv_sem=fwd_recv.at[g],
            device_id=sibling,
            device_id_type=MESH,
        )

    def pass_on(g):
        whole(att.at[g, rows_at(mp_i, rows)], o_recv.at[g]).wait()
        forward(g).start()

    def project(g):
        whole(wbuf.at[g], w_sem.at[g]).wait()
        whole(att.at[g, rows_at(1 - mp_i, rows)], fwd_recv.at[g]).wait()
        tile = 2 * HEAD_DIM

        def step(i, carry):
            at = rows_at(i, tile)
            part = jnp.dot(
                att[g], wbuf[g, :, at], preferred_element_type=jnp.float32
            )
            acc[:, at] += part
            return carry

        lax.fori_loop(0, columns // tile, step, 0)

    send_group(0)
    if groups > 1:
        send_group(1)
    load_res.start()
    for g in range(groups):

        def start_load(p, carry, g=g):
            load_weight(g, p).start()
            return carry

        lax.fori_loop(0, n, start_load, 0)
    whole(counts.at[pl.ds(0, 8 * (n - 1))], cnt_recv).wait()
    sums = counts[pl.ds(0, 8), :]
    for r in range(1, n):
        sums = sums + counts[pl.ds(8 * r, 8), :]
    totals = [sums[k : k + 1, 0:1] for k in range(VIDEOS - 1)]

    acc[...] = jnp.zeros_like(acc)

    def group(g, carry):
        whole(qkv.at[g], qkv_recv.at[g]).wait()

        @pl.when(g + 2 < groups)
        def _():
            send_group(g + 2)

        for part in range(2):
            attention(g, totals, part)
            send_back(g, part)

        @pl.when(g >= 1)
        def _():
            pass_on(g - 1)

        @pl.when(g >= 2)
        def _():
            project(g - 2)

        return carry

    lax.fori_loop(0, groups, group, 0)
    if groups >= 2:
        project(groups - 2)
    pass_on(groups - 1)
    project(groups - 1)

    load_res.wait()
    gate = mod_ref[0:1, :]
    shift = mod_ref[1:2, :]
    scale = 1.0 + mod_ref[2:3, :]
    high = acc.shape[0]
    tile = 64
    side = lax.broadcasted_iota(jnp.int32, (tile, 128), 1) < 64

    def gated(i, carry):
        at = rows_at(i, tile)
        stream = res[at, :].astype(jnp.float32) + gate * acc[at, :]
        acc[at, :] = stream
        hid[at, :] = stream.astype(jnp.bfloat16)
        row_sum = jnp.sum(stream, axis=1, keepdims=True)
        row_sq = jnp.sum(stream * stream, axis=1, keepdims=True)
        stat_mine[at, :] = jnp.where(side, row_sum, row_sq)
        return carry

    lax.fori_loop(0, high // tile, gated, 0)
    stats = pltpu.make_async_remote_copy(
        src_ref=stat_mine,
        dst_ref=stat_other,
        send_sem=stat_send,
        recv_sem=stat_recv,
        device_id=sibling,
        device_id_type=MESH,
    )
    stats.start()
    store_hid = pltpu.make_async_copy(hid, hid_ref, out_sem.at[0])
    store_hid.start()
    stats.wait_recv()

    def normed(i, carry):
        at = rows_at(i, tile)
        both = stat_mine[at, :] + stat_other[at, :]
        mean = both[:, 0:1] / width
        var = both[:, 64:65] / width - mean * mean
        stream = acc[at, :]
        result = (stream - mean) * lax.rsqrt(var + 1e-06) * scale + shift
        mlp[at, :] = result.astype(jnp.bfloat16)
        return carry

    lax.fori_loop(0, high // tile, normed, 0)
    store_mlp = pltpu.make_async_copy(mlp, mlp_ref, out_sem.at[1])
    store_mlp.start()

    stats.wait_send()
    whole(counts.at[pl.ds(0, 8 * (n - 1))], cnt_send).wait()
    for g in range(groups):
        whole(qkv.at[g, :, pl.ds(0, rows * (n - 1))], qkv_send.at[g]).wait()
        whole(obuf.at[g, pl.ds(0, rows * (n - 1))], o_send.at[g]).wait()
        forward(g).wait_send()
    store_hid.wait()
    store_mlp.wait()


def fused(n, mp_n, residual, queries, keys, values, video_ids, timestep, modulation, out_weight):
    mod_rows = lax.dynamic_index_in_dim(modulation, timestep[0], 0, keepdims=False)
    rows, width = queries.shape
    high, columns = residual.shape
    tokens = rows * n
    groups = width // HEAD_DIM // n
    bf16 = jnp.bfloat16
    dma = pltpu.SemaphoreType.DMA
    anywhere = pl.BlockSpec(memory_space=pl.ANY)
    vmem = pl.BlockSpec(memory_space=pltpu.VMEM)
    out = jax.ShapeDtypeStruct(residual.shape, bf16)
    return pl.pallas_call(
        functools.partial(fused_kernel, n, mp_n, width),
        out_shape=(out, out),
        in_specs=[anywhere, anywhere, anywhere, vmem, vmem, anywhere, anywhere],
        out_specs=(anywhere, anywhere),
        scratch_shapes=[
            pltpu.VMEM((groups, 3, tokens, HEAD_DIM), bf16),
            pltpu.VMEM((groups, tokens, HEAD_DIM), bf16),
            pltpu.VMEM((groups, high, n * HEAD_DIM), bf16),
            pltpu.VMEM((groups, n * HEAD_DIM, columns), bf16),
            pltpu.VMEM((high, columns), bf16),
            pltpu.VMEM((high, columns), jnp.float32),
            pltpu.VMEM((high, columns), bf16),
            pltpu.VMEM((high, columns), bf16),
            pltpu.VMEM((8 * n, 128), jnp.float32),
            pltpu.VMEM((high, 128), jnp.float32),
            pltpu.VMEM((high, 128), jnp.float32),
            dma((groups,)), dma((groups,)), dma((groups,)), dma((groups,)),
            dma((groups,)), dma((groups,)),
            dma, dma, dma, dma, dma((groups,)), dma, dma((2,)),
        ],
        compiler_params=pltpu.CompilerParams(
            collective_id=0, has_side_effects=True, vmem_limit_bytes=52 * 2**20
        ),
    )(queries, keys, values, video_ids.reshape(1, rows), mod_rows, residual, out_weight)


def attend(carry, q_rows, q_ids, key_rows, value_rows, key_ids):
    top, total, summed = carry
    rows = q_rows.shape[0]
    count = key_rows.shape[0]
    heads = q_rows.shape[1] // HEAD_DIM
    factor = 1.0 / HEAD_DIM**0.5
    q_heads = q_rows.reshape(rows, heads, HEAD_DIM)
    k_heads = key_rows.reshape(count, heads, HEAD_DIM)
    v_heads = value_rows.reshape(count, heads, HEAD_DIM)
    same = (q_ids[:, None] == key_ids[None, :])[None]
    new_top, new_total, new_summed = ([], [], [])
    for first in range(0, heads, 3):
        score = (
            jnp.einsum(
                "thd,nhd->htn",
                q_heads[:, first : first + 3],
                k_heads[:, first : first + 3],
                preferred_element_type=jnp.float32,
            )
            * factor
        )
        score = jnp.where(same, score, -1e30)
        old_top = top[first : first + 3]
        peak = jnp.maximum(old_top, jnp.max(score, axis=2))
        weight = jnp.where(same, jnp.exp(score - peak[:, :, None]), 0.0)
        new_top.append(peak)
        new_total.append(jnp.sum(weight, axis=2))
        part_sum = jnp.einsum(
            "htn,nhd->htd",
            weight.astype(jnp.bfloat16),
            v_heads[:, first : first + 3],
            preferred_element_type=jnp.float32,
        )
        new_summed.append(part_sum)
    return (
        jnp.concatenate(new_top, 0),
        jnp.concatenate(new_total, 0),
        jnp.concatenate(new_summed, 0),
    )


def attend_maybe(carry, q_rows, q_ids, key_rows, value_rows, key_ids):
    return attend(carry, q_rows, q_ids, key_rows, value_rows, key_ids)


def start_state(q_rows):
    rows = q_rows.shape[0]
    heads = q_rows.shape[1] // HEAD_DIM
    return (
        jnp.full((heads, rows), -1e30, jnp.float32),
        jnp.zeros((heads, rows), jnp.float32),
        jnp.zeros((heads, rows, HEAD_DIM), jnp.float32),
    )


def finish(state, q_rows):
    top, total, summed = state
    rows = q_rows.shape[0]
    heads = q_rows.shape[1] // HEAD_DIM
    result = summed / total[:, :, None]
    return result.transpose(1, 0, 2).reshape(rows, heads * HEAD_DIM).astype(jnp.bfloat16)


def local(residual, queries, keys, values, video_ids, timestep, modulation, out_weight):
    steps_count = modulation.shape[0]
    picker = (jnp.arange(steps_count, dtype=jnp.int32) == timestep[0]).astype(jnp.float32)
    mod_rows = jnp.einsum("s,scd->cd", picker, modulation, precision=lax.Precision.HIGHEST)
    gate = mod_rows[0]
    shift = mod_rows[1]
    scale = mod_rows[2]
    width = queries.shape[1]
    state = attend_maybe(
        start_state(queries),
        queries,
        video_ids,
        lax.all_gather(keys, ("seq", "mp"), axis=0, tiled=True),
        lax.all_gather(values, ("seq", "mp"), axis=0, tiled=True),
        lax.all_gather(video_ids, ("seq", "mp"), axis=0, tiled=True),
    )
    attended = finish(state, queries)
    projected = jnp.dot(
        lax.all_gather(attended, "mp", axis=0, tiled=True),
        out_weight,
        preferred_element_type=jnp.float32,
    )
    stream = residual.astype(jnp.float32) + gate[None, :] * projected
    row_sum = jnp.sum(stream, axis=1, keepdims=True)
    row_sq = jnp.sum(stream * stream, axis=1, keepdims=True)
    row_sum, row_sq = lax.psum((row_sum, row_sq), "mp")
    mean = row_sum / width
    var = row_sq / width - mean * mean
    normed = (stream - mean) * lax.rsqrt(var + 1e-06) * (1.0 + scale[None, :]) + shift[None, :]
    return (stream.astype(jnp.bfloat16), normed.astype(jnp.bfloat16))


def choose(mesh):
    seq_n, mp_n = mesh.shape["seq"], mesh.shape["mp"]
    n = seq_n * mp_n

    def run(*arrays):
        queries = arrays[1]
        rows, width = queries.shape
        if mp_n == 2 and width // HEAD_DIM % n == 0 and rows % 64 == 0 and rows * n % 512 == 0:
            return fused(n, mp_n, *arrays)
        return local(*arrays)

    return run


def solution(mesh):
    return jax.shard_map(
        choose(mesh),
        mesh=mesh,
        in_specs=(
            P(("dp", "seq"), "mp"),
            P(("dp", "seq", "mp"), None),
            P(("dp", "seq", "mp"), None),
            P(("dp", "seq", "mp"), None),
            P(("dp", "seq", "mp")),
            P("dp"),
            P(None, None, "mp"),
            P(None, "mp"),
        ),
        out_specs=(P(("dp", "seq"), "mp"), P(("dp", "seq"), "mp")),
        check_vma=False,
    )
```
